32 devices in a mesh: day: 2 (over x), chan: 16 (over z, y, core).
Axes of the slice: x: 2, y: 2, z: 4, core: 2. Of those that a mesh axis runs over, the one named last changes fastest.
Arguments:
- records: bfloat16 [1024, 8, 3000], P(('day', 'chan')), parts along dimension 0, may hold values from -6 to 6
- live_mask: int32 [1024], P(('day', 'chan')), parts along dimension 0, may hold values 0 or 1
- offsets: int32 [16], replicated, may hold values from 1 to 511, as said below
Outputs:
- correlations: bfloat16 [1024, 16, 2048], P(('day', 'chan')), parts along dimension 0
The draws below stay inside these ranges and needn't reach their ends.
There are 2 independent parts, one for each index of `day`. The reference program is written for one: setup_inputs(seed, part) draws one part's arguments, and reference() takes and returns one part's arrays. A program takes and returns all parts, laid end to end along the dimension named above; an argument that names none is the same for every part. Nothing has to cross between parts.
Inputs may be any that keep to these rules, and one draw needn't show every extreme that they name: offsets[k] lies between k * 32 + 1 and (k + 1) * 32, and the last one equals 511.
All inputs are finite; a program needn't handle non-finite values. No bound on the sum of `live_mask` on one device may be relied on, other than what follows from the above.
Results may differ from the reference program's by a relative error of at most 0.0076.
Values may be sent and summed in bfloat16 or wider, within the bound.
No kernel may reach another device: no remote copies, remote signals or barrier semaphores. Data moves between devices by JAX's collectives and lax.ppermute only.
A program may use at most 128 MiB of HBM per device.

```python
import math
import jax
import jax.numpy as jnp
from jax import lax

W = 8
L = 3000
F = 512
F0 = 6
LAGS = 2048
BAND = 512
K = 16
CH_TOTAL = 512


def draw_offsets(key, part):
    stride = BAND // K
    index = jnp.arange(K, dtype=jnp.int32)
    base = index * stride + 1
    jitter = jax.random.randint(key, (K,), 0, stride, dtype=jnp.int32)
    jitter = jnp.where(index == K - 1, stride - 2, jitter)
    return (base + jitter).astype(jnp.int32)


def place_ends(entries, own_key, low, largest):
    longest = entries.shape.index(max(entries.shape))
    spots = []
    for shift in (0, 1):
        where = [jax.random.randint(jax.random.fold_in(own_key, axis), (), 0, length) for axis, length in enumerate(entries.shape)]
        where[longest] = (where[longest] + shift) % entries.shape[longest]
        spots.append(tuple(where))
    return entries.at[spots[0]].set(low).at[spots[1]].set(largest)


def shard_levels(rng, dims, cuts, low, high):
    level = 1.0
    for dim, shards_of in cuts:
        steps = jax.random.uniform(jax.random.fold_in(jax.random.fold_in(rng, 6), dim), (shards_of,), jnp.float32, low / len(cuts), high / len(cuts))
        level = level * jnp.repeat(jnp.exp(steps), dims[dim] // shards_of).reshape((-1,) + (1,) * (len(dims) - 1 - dim))
    return level


def normal_values(rng, shape, deviation, bound, shards=(), kind=jnp.bfloat16):
    level = shard_levels(rng, shape, shards, -0.22, 0.18) if shards else 1.0
    drawn = jax.random.normal(rng, shape, jnp.float32) * deviation * level
    return jnp.minimum(jnp.maximum(drawn, -bound), bound).astype(kind)


def setup_inputs(seed: int = 0, part: int = 0) -> dict:
    streams_of = jax.random.split(jax.random.key(seed), 4)
    part_keys = jax.random.split(jax.random.fold_in(streams_of[3], part), 4)
    return {
        "records": normal_values(part_keys[0], (CH_TOTAL, W, L), 1.0, 6.0, ((0, 16),)),
        "live_mask": place_ends((jax.random.randint(part_keys[1], (CH_TOTAL,), 0, 10) < 9).astype(jnp.int32), jax.random.fold_in(part_keys[1], 1), 0, 1),
        "offsets": draw_offsets(jax.random.fold_in(streams_of[3], 71), part),
    }


def forward_table(length):
    samples = jnp.arange(length, dtype=jnp.int32)
    freqs = F0 + jnp.arange(F, dtype=jnp.int32)
    phase = jnp.mod(samples[:, None] * freqs[None, :], length).astype(jnp.float32)
    angle = 2.0 * math.pi / length * phase
    return jnp.concatenate([jnp.cos(angle), -jnp.sin(angle)], axis=1).astype(jnp.bfloat16)

def inverse_table(length):
    freqs = F0 + jnp.arange(F, dtype=jnp.int32)
    shifts = jnp.arange(LAGS, dtype=jnp.int32) - LAGS // 2
    phase = jnp.mod(freqs[:, None] * shifts[None, :], length).astype(jnp.float32)
    angle = 2.0 * math.pi / length * phase
    return jnp.concatenate([jnp.cos(angle), -jnp.sin(angle)], axis=0).astype(jnp.bfloat16)

def whiten(records, live_mask):
    count, windows, length = records.shape
    table = forward_table(length)
    spectrum = jnp.dot(records.reshape(count * windows, length), table, preferred_element_type=jnp.float32)
    power = lax.optimization_barrier(jnp.mean(spectrum * spectrum, axis=1, keepdims=True))
    gain = jnp.repeat(live_mask.astype(jnp.float32), windows)[:, None]
    white = spectrum * (gain * lax.rsqrt(power + 1e-06))
    return white.astype(jnp.bfloat16).reshape(count, windows, 2, spectrum.shape[1] // 2)

def stacked_cross(local_spec, extended, offsets):
    row_count, windows, paired, bin_count = local_spec.shape
    first = local_spec.astype(jnp.float32)

    def single(offset_value):
        partner = lax.dynamic_slice_in_dim(extended, offset_value, row_count, 0).astype(jnp.float32)
        real_part = lax.optimization_barrier(jnp.sum(first[:, :, 0] * partner[:, :, 0] + first[:, :, 1] * partner[:, :, 1], axis=1))
        imag_part = lax.optimization_barrier(jnp.sum(first[:, :, 1] * partner[:, :, 0] - first[:, :, 0] * partner[:, :, 1], axis=1))
        return jnp.stack([real_part, imag_part], axis=1) / float(windows)

    def grouped(group):
        return jax.vmap(single)(group)
    result = lax.map(grouped, offsets.reshape(-1, 8))
    result = result.reshape(offsets.shape[0], row_count, 2, bin_count)
    return jnp.transpose(result, (1, 0, 2, 3)).astype(jnp.bfloat16)

def lag_transform(cross, length):
    count, pairs, paired, bin_count = cross.shape
    table = inverse_table(length)
    result = jnp.dot(cross.reshape(count * pairs, 2 * bin_count), table, preferred_element_type=jnp.float32)
    result = result * (1.0 / math.sqrt(bin_count))
    return result.reshape(count, pairs, table.shape[1]).astype(jnp.bfloat16)

def reference(records, live_mask, offsets):
    spectra = whiten(records, live_mask)
    padding = jnp.zeros((BAND,) + spectra.shape[1:], jnp.bfloat16)
    extended = jnp.concatenate([spectra, padding], axis=0)
    cross = stacked_cross(spectra, extended, offsets)
    return lag_transform(cross, records.shape[2])
```

```python
import functools
import math

import jax
import jax.numpy as jnp
import ml_dtypes
import numpy as np
from jax import lax
from jax.experimental import pallas as pl
from jax.experimental.pallas import tpu as pltpu
from jax.sharding import PartitionSpec as P

F = 512
F0 = 6
LAGS = 2048
BAND = 512
TEAM = 4
HALVES = 2
LANES = 128
BINS = F // (TEAM * HALVES)
VMEM = 56 * 1024 * 1024


def column_order():
    bins = np.arange(F).reshape(TEAM, HALVES, 1, BINS)
    parts = np.arange(2).reshape(1, 1, 2, 1) * F
    return (bins + parts).reshape(-1)


def tables(length):
    freqs = F0 + np.arange(F, dtype=np.int64)
    unit = np.float32(2.0 * math.pi / length)

    def cut(phase):
        angle = unit * np.mod(phase, length).astype(np.float32)
        return np.cos(angle), -np.sin(angle)

    order = column_order()
    forward = np.concatenate(cut(np.arange(length)[:, None] * freqs[None, :]), axis=1)[:, order]
    forward = forward.reshape(length, TEAM, 2 * F // TEAM).transpose(1, 0, 2)
    shifts = np.arange(LAGS, dtype=np.int64) - LAGS // 2
    inverse = np.concatenate(cut(freqs[:, None] * shifts[None, :]), axis=0)[order]
    inverse = inverse.reshape(TEAM, 2 * F // TEAM, LAGS)
    return forward.astype(ml_dtypes.bfloat16), inverse.astype(ml_dtypes.bfloat16)


def spectra_kernel(windows, records, table, live, own0, own1, far0, far1, spec, power):
    step = pl.program_id(0)
    rows = records.shape[0]
    count = rows // windows
    block = jnp.dot(records[...], table[0], preferred_element_type=jnp.float32)
    for half in range(HALVES):
        spec[step * HALVES + half] = block[:, half * LANES : (half + 1) * LANES]
    squares = jnp.sum(block * block, axis=1, keepdims=True)
    total = jnp.where(step == 0, 0.0, power[...]) + squares
    power[...] = total

    @pl.when(step == TEAM - 1)
    def _():
        me = lax.rem(lax.axis_index("chan"), TEAM)
        channel = lax.broadcasted_iota(jnp.int32, (rows, count), 0) // windows
        lane = lax.broadcasted_iota(jnp.int32, (rows, count), 1)
        mask = jnp.where(channel == lane, live[...].astype(jnp.float32), 0.0)
        gain = jnp.sum(mask, axis=1, keepdims=True)
        scale = gain * lax.rsqrt(total * (1.0 / (2 * F)) + 1e-06)
        for part in range(TEAM * HALVES):
            spec[part] = spec[part] * scale
        for d in range(TEAM):
            quarter = jnp.bitwise_xor(me, d)
            for half, out in enumerate((own0, own1) if d < 2 else (far0, far1)):
                for w in range(windows):
                    piece = spec[quarter * HALVES + half, pl.ds(w, count, stride=windows), :]
                    out[d % 2, w * count : (w + 1) * count, :] = piece.astype(jnp.bfloat16)


def spectra(records, live_mask, table):
    count, windows, length = records.shape
    rows = count * windows
    width = 2 * F // TEAM
    piece = jax.ShapeDtypeStruct((2, rows, LANES), jnp.bfloat16)
    whole = pl.BlockSpec((2, rows, LANES), lambda i: (0, 0, 0))
    return pl.pallas_call(
        functools.partial(spectra_kernel, windows),
        grid=(TEAM,),
        in_specs=[
            pl.BlockSpec((rows, length), lambda i: (0, 0)),
            pl.BlockSpec((1, length, width), lambda i: (i, 0, 0)),
            pl.BlockSpec((1, count), lambda i: (0, 0)),
        ],
        out_specs=[whole] * 4,
        out_shape=[piece] * 4,
        scratch_shapes=[
            pltpu.VMEM((TEAM * HALVES, rows, LANES), jnp.float32),
            pltpu.VMEM((rows, 1), jnp.float32),
        ],
        compiler_params=pltpu.CompilerParams(vmem_limit_bytes=VMEM),
        name="spectra",
    )(records.reshape(rows, length), table, live_mask.reshape(1, count))


def cross_kernel(windows, count, first, last, low, planes, offsets, *refs):
    given, (near, far, side, extended, paired) = refs[: 4 * (planes + 1)], refs[4 * (planes + 1) :]
    me = lax.rem(lax.axis_index("chan"), TEAM)
    span = TEAM * count
    number = last - first
    blocks = [jnp.bitwise_xor(me, d) for d in range(TEAM)]

    def pieces(plane):
        own, own_swapped, across, across_swapped = given[4 * plane : 4 * plane + 4]
        return (own, own_swapped, across, across_swapped)

    for d, ref in enumerate(pieces(0)):
        for w in range(windows):
            side[w, d * count : (d + 1) * count, :] = ref[0, w * count : (w + 1) * count, :].astype(jnp.float32)
    for plane in range(planes):
        for d, ref in enumerate(pieces(plane + 1)):
            start = pl.multiple_of(plane * span + blocks[d] * count, count)
            for w in range(windows):
                extended[w, pl.ds(start, count), :] = ref[0, w * count : (w + 1) * count, :].astype(jnp.float32)
    tail = extended.shape[1] - planes * span
    if tail:
        extended[:, planes * span :, :] = jnp.zeros((windows, tail, LANES), jnp.float32)

    lane = lax.broadcasted_iota(jnp.int32, (8, LANES), 1)
    real_lane = lane < BINS
    sign = jnp.where(real_lane, 1.0 / windows, -1.0 / windows)

    def group(step, carry):
        at = pl.multiple_of(step * 8, 8)
        d = step // (count // 8)
        within = lax.rem(step, count // 8) * 8
        channel = jnp.bitwise_xor(me, d) * count + within
        straight, turned = [], []
        for w in range(windows):
            value = side[w, pl.ds(at, 8), :]
            straight.append(value * (1.0 / windows))
            turned.append(pltpu.roll(value, BINS, 1) * sign)
        for j in range(number):
            place = channel + offsets[first + j] - low * span
            real_part, imag_part = None, None
            for w in range(windows):
                partner = extended[w, pl.ds(place, 8), :]
                r, i = straight[w] * partner, turned[w] * partner
                real_part = r if w == 0 else real_part + r
                imag_part = i if w == 0 else imag_part + i
            real_part = real_part + pltpu.roll(real_part, BINS, 1)
            imag_part = imag_part + pltpu.roll(imag_part, BINS, 1)
            both = jnp.where(real_lane, real_part, imag_part)
            paired[d, pl.ds(within * number + j, 8, stride=number), :] = both
        return carry

    lax.fori_loop(0, span // 8, group, 0)
    for d in range(TEAM):
        (near if d < 2 else far)[d % 2] = paired[d].astype(jnp.bfloat16)


def cross(windows, count, first, last, offsets, team_planes):
    span = TEAM * count
    stride = BAND // offsets.shape[0]
    low = (first * stride + 1) // span
    high = (span - 1 + last * stride) // span
    partners = [team_planes[p] for p in range(low, min(high, len(team_planes) - 1) + 1)]
    rows = windows * count
    halves = [0, 1, 0, 1] * (len(partners) + 1)
    number = last - first
    out = jax.ShapeDtypeStruct((2, count * number, LANES), jnp.bfloat16)
    return pl.pallas_call(
        functools.partial(cross_kernel, windows, count, first, last, low, len(partners)),
        grid=(1,),
        in_specs=[pl.BlockSpec(memory_space=pltpu.SMEM)]
        + [pl.BlockSpec((1, rows, LANES), lambda i, h=h: (h, 0, 0)) for h in halves],
        out_specs=[pl.BlockSpec((2, count * number, LANES), lambda i: (0, 0, 0))] * 2,
        out_shape=[out] * 2,
        scratch_shapes=[
            pltpu.VMEM((windows, span, LANES), jnp.float32),
            pltpu.VMEM((windows, (high - low + 1) * span, LANES), jnp.float32),
            pltpu.VMEM((TEAM, count * number, LANES), jnp.float32),
        ],
        compiler_params=pltpu.CompilerParams(vmem_limit_bytes=VMEM),
        name="cross",
    )(offsets, *[piece for plane in [team_planes[0]] + partners for piece in plane])


def lag_kernel(count, groups, *refs):
    given, table, out = refs[:-2], refs[-2], refs[-1]
    me = lax.rem(lax.axis_index("chan"), TEAM)
    columns = []
    for g in range(groups):
        total = None
        for d in range(TEAM):
            quarter = jnp.bitwise_xor(me, d)
            left = jnp.concatenate([given[(g * HALVES + h) * TEAM + d][0] for h in range(HALVES)], axis=1)
            term = jnp.dot(left, table[quarter], preferred_element_type=jnp.float32)
            total = term if d == 0 else total + term
        columns.append(total.reshape(count, total.shape[0] // count, total.shape[1]))
    result = jnp.concatenate(columns, axis=1) * (1.0 / math.sqrt(F))
    out[...] = result.astype(jnp.bfloat16)


def lags(count, number, parts, table):
    tile = 512
    arrays = [piece for group in parts for half in group for piece in half]
    halves = [0, 1, 0, 1] * (len(arrays) // 4)
    return pl.pallas_call(
        functools.partial(lag_kernel, count, len(parts)),
        grid=(LAGS // tile,),
        in_specs=[
            pl.BlockSpec((1,) + a.shape[1:], lambda i, h=h: (h, 0, 0)) for a, h in zip(arrays, halves)
        ]
        + [pl.BlockSpec((TEAM, table.shape[1], tile), lambda i: (0, 0, i))],
        out_specs=pl.BlockSpec((count, number, tile), lambda i: (0, 0, i)),
        out_shape=jax.ShapeDtypeStruct((count, number, LAGS), jnp.bfloat16),
        compiler_params=pltpu.CompilerParams(vmem_limit_bytes=VMEM),
        name="lags",
    )(*arrays, table)


def solution(mesh):
    ring = mesh.shape["chan"]
    if ring % TEAM:
        raise ValueError("chan")

    def swapped(value, by):
        return lax.ppermute(value, "chan", [(i, i ^ by) for i in range(ring)])

    def down(value, hops):
        pairs = [(i, i - TEAM) for i in range(TEAM, ring) if i // TEAM + hops - 1 < ring // TEAM]
        return lax.ppermute(value, "chan", pairs)

    def shards(records, live_mask, offsets):
        count, windows, length = records.shape
        span = TEAM * count
        number = offsets.shape[0]
        forward, inverse = tables(length)
        own0, own1, far0, far1 = spectra(records, live_mask, jnp.asarray(forward))
        across0, across1 = swapped(far0, 2), swapped(far1, 2)
        reach = min((span + BAND - 2) // span, ring // TEAM - 1)
        chunks = [[[own0, across0], [own1, across1]]]
        for hops in range(1, reach + 1):
            previous = chunks[-1]
            chunks.append([[down(c, hops) for c in half] for half in previous])
        planes = [
            [[piece for c in half for piece in (c, swapped(c, 1))] for half in chunk] for chunk in chunks
        ]
        parts = []
        for first, last in ((0, number // 2), (number // 2, number)):
            group = []
            for half in range(HALVES):
                near, far = cross(windows, count, first, last, offsets, [p[half] for p in planes])
                back = swapped(far, 2)
                group.append([near, swapped(near, 1), back, swapped(back, 1)])
            parts.append(group)
        return lags(count, number, parts, jnp.asarray(inverse))

    in_specs = (P(("day", "chan"), None, None), P(("day", "chan")), P())
    out_specs = P(("day", "chan"), None, None)
    return jax.shard_map(shards, mesh=mesh, in_specs=in_specs, out_specs=out_specs, check_vma=False)
```

```python
import functools
import math

import jax
import jax.numpy as jnp
import ml_dtypes
import numpy as np
from jax import lax
from jax.experimental import pallas as pl
from jax.experimental.pallas import tpu as pltpu
from jax.sharding import PartitionSpec as P

F = 512
F0 = 6
LAGS = 2048
BAND = 512
TEAM = 4
HALVES = 2
LANES = 128
BINS = F // (TEAM * HALVES)
QUADRANTS = 4

MIB = 1024 * 1024


def busy(microseconds):
    return pl.CostEstimate(flops=int(microseconds * 1.1535e9), bytes_accessed=0, transcendentals=0)


def column_order():
    bins = np.arange(F)[np.argsort((F0 + np.arange(F)) % TEAM, kind="stable")].reshape(TEAM, HALVES, 1, BINS)
    parts = np.arange(2).reshape(1, 1, 2, 1) * F
    return (bins + parts).reshape(-1)


def tables(length):
    freqs = F0 + np.arange(F, dtype=np.int64)
    unit = np.float32(2.0 * math.pi / length)

    def cut(phase):
        angle = unit * np.mod(phase, length).astype(np.float32)
        return np.cos(angle), -np.sin(angle)

    order = column_order()
    part = length // QUADRANTS
    forward = np.concatenate(cut(np.arange(part)[:, None] * freqs[None, :]), axis=1)[:, order]
    forward = forward.reshape(part, TEAM, 2 * F // TEAM).transpose(1, 0, 2)
    shifts = np.arange(LAGS, dtype=np.int64) - LAGS // 2
    inverse = np.concatenate(cut(freqs[:, None] * shifts[None, :]), axis=0)[order]
    inverse = inverse.reshape(TEAM, 2 * F // TEAM, LAGS)
    return forward.astype(ml_dtypes.bfloat16), inverse.astype(ml_dtypes.bfloat16)


def spectra_kernel(windows, records_hbm, table_hbm, live, own0, own1, far0, far1, records, table, spec, sems):
    rows, length = records.shape
    count = rows // windows
    part = length // QUADRANTS
    copies = [pltpu.make_async_copy(records_hbm, records, sems.at[0])]
    copies += [pltpu.make_async_copy(table_hbm.at[c], table.at[c], sems.at[1 + c]) for c in range(TEAM)]
    for copy in copies:
        copy.start()
    me = lax.rem(lax.axis_index("chan"), TEAM)
    channel = lax.broadcasted_iota(jnp.int32, (rows, count), 0) // windows
    lane = lax.broadcasted_iota(jnp.int32, (rows, count), 1)
    mask = jnp.where(channel == lane, live[...].astype(jnp.float32), 0.0)
    gain = jnp.sum(mask, axis=1, keepdims=True)
    real_lane = lax.broadcasted_iota(jnp.int32, (rows, LANES), 1) < BINS
    copies[0].wait()
    quadrants = [records[:, q * part : (q + 1) * part] for q in range(QUADRANTS)]
    squares = jnp.zeros((rows, LANES), jnp.float32)
    for c in range(TEAM):
        copies[1 + c].wait()
        terms = [jnp.dot(x, table[c], preferred_element_type=jnp.float32) for x in quadrants]
        for half in range(HALVES):
            t0, t1, t2, t3 = (t[:, half * LANES : (half + 1) * LANES] for t in terms)
            if c == 0:
                value = (t0 + t2) + (t1 + t3)
            elif c == 2:
                value = (t0 + t2) - (t1 + t3)
            else:
                turned = pltpu.roll(t1 - t3, BINS, 1)
                value = (t0 - t2) + jnp.where(real_lane == (c == 1), turned, -turned)
            spec[c * HALVES + half] = value
            squares = squares + value * value
    power = jnp.sum(squares, axis=1, keepdims=True)
    scale = gain * lax.rsqrt(power * (1.0 / (2 * F)) + 1e-06)
    for k in range(TEAM * HALVES):
        spec[k] = spec[k] * scale
    for half, outs in enumerate(((own0, far0), (own1, far1))):
        for d in range(TEAM):
            c = jnp.bitwise_xor(me, d)
            for w in range(windows):
                piece = spec[c * HALVES + half, pl.ds(w, count, stride=windows), :]
                outs[d // 2][d % 2, w * count : (w + 1) * count, :] = piece.astype(jnp.bfloat16)


def spectra(records, live_mask, table):
    count, windows, length = records.shape
    rows = count * windows
    return pl.pallas_call(
        functools.partial(spectra_kernel, windows),
        in_specs=[
            pl.BlockSpec(memory_space=pl.ANY),
            pl.BlockSpec(memory_space=pl.ANY),
            pl.BlockSpec(memory_space=pltpu.VMEM),
        ],
        out_specs=[pl.BlockSpec(memory_space=pltpu.VMEM)] * 4,
        out_shape=[pltpu.VMEM((2, rows, LANES), jnp.bfloat16)] * 4,
        scratch_shapes=[
            pltpu.VMEM((rows, length), jnp.bfloat16),
            pltpu.VMEM(table.shape, jnp.bfloat16),
            pltpu.VMEM((TEAM * HALVES, rows, LANES), jnp.float32),
            pltpu.SemaphoreType.DMA((1 + TEAM,)),
        ],
        compiler_params=pltpu.CompilerParams(vmem_limit_bytes=20 * MIB),
        cost_estimate=busy(3.0),
        name="spectra",
    )(records.reshape(rows, length), table, live_mask.reshape(1, count))


def cross_kernel(windows, count, first, last, low, planes, offsets, *refs):
    given, (near, far, side, extended, paired) = refs[: 4 * (planes + 1)], refs[4 * (planes + 1) :]
    me = lax.rem(lax.axis_index("chan"), TEAM)
    span = TEAM * count
    number = last - first
    blocks = [jnp.bitwise_xor(me, d) for d in range(TEAM)]

    def pieces(plane):
        own, own_swapped, across, across_swapped = given[4 * plane : 4 * plane + 4]
        return (own, own_swapped, across, across_swapped)

    for d, ref in enumerate(pieces(0)):
        for w in range(windows):
            side[w, d * count : (d + 1) * count, :] = ref[d % 2, w * count : (w + 1) * count, :].astype(jnp.float32)
    for plane in range(planes):
        for d, ref in enumerate(pieces(plane + 1)):
            start = pl.multiple_of(plane * span + blocks[d] * count, count)
            for w in range(windows):
                extended[w, pl.ds(start, count), :] = ref[d % 2, w * count : (w + 1) * count, :].astype(jnp.float32)
    tail = extended.shape[1] - planes * span
    if tail:
        extended[:, planes * span :, :] = jnp.zeros((windows, tail, LANES), jnp.float32)

    lane = lax.broadcasted_iota(jnp.int32, (8, LANES), 1)
    real_lane = lane < BINS
    sign = jnp.where(real_lane, 1.0 / windows, -1.0 / windows)

    def group(step, carry):
        at = pl.multiple_of(step * 8, 8)
        d = step // (count // 8)
        within = lax.rem(step, count // 8) * 8
        channel = jnp.bitwise_xor(me, d) * count + within
        straight, turned = [], []
        for w in range(windows):
            value = side[w, pl.ds(at, 8), :]
            straight.append(value * (1.0 / windows))
            turned.append(pltpu.roll(value, BINS, 1) * sign)
        for j in range(number):
            place = channel + offsets[first + j] - low * span
            real_part, imag_part = None, None
            for w in range(windows):
                partner = extended[w, pl.ds(place, 8), :]
                r, i = straight[w] * partner, turned[w] * partner
                real_part = r if w == 0 else real_part + r
                imag_part = i if w == 0 else imag_part + i
            folded = pltpu.roll(jnp.where(real_lane, imag_part, real_part), BINS, 1)
            both = jnp.where(real_lane, real_part, imag_part) + folded
            paired[d, pl.ds(within * number + j, 8, stride=number), :] = both
        return carry

    lax.fori_loop(0, span // 8, group, 0, unroll=2)
    for d in range(TEAM):
        (near if d < 2 else far)[d % 2] = paired[d].astype(jnp.bfloat16)


def cross(windows, count, first, last, offsets, team_planes):
    span = TEAM * count
    stride = BAND // offsets.shape[0]
    low = (first * stride + 1) // span
    high = (span - 1 + last * stride) // span
    partners = [team_planes[p] for p in range(low, min(high, len(team_planes) - 1) + 1)]
    number = last - first
    vmem = pl.BlockSpec(memory_space=pltpu.VMEM)
    return pl.pallas_call(
        functools.partial(cross_kernel, windows, count, first, last, low, len(partners)),
        in_specs=[pl.BlockSpec(memory_space=pltpu.SMEM)] + [vmem] * (4 * len(partners) + 4),
        out_specs=[vmem] * 2,
        out_shape=[pltpu.VMEM((2, count * number, LANES), jnp.bfloat16)] * 2,
        scratch_shapes=[
            pltpu.VMEM((windows, span, LANES), jnp.float32),
            pltpu.VMEM((windows, (high - low + 1) * span, LANES), jnp.float32),
            pltpu.VMEM((TEAM, count * number, LANES), jnp.float32),
        ],
        compiler_params=pltpu.CompilerParams(vmem_limit_bytes=8 * MIB),
        cost_estimate=busy(2.5),
        name="cross",
    )(offsets, *[piece for plane in [team_planes[0]] + partners for piece in plane])


def lag_sum(given, table, columns):
    me = lax.rem(lax.axis_index("chan"), TEAM)
    total = None
    for d in range(TEAM):
        left = jnp.concatenate([given[h * TEAM + d][d % 2] for h in range(HALVES)], axis=1)
        term = jnp.dot(left, table[jnp.bitwise_xor(me, d), :, columns], preferred_element_type=jnp.float32)
        total = term if d == 0 else total + term
    return total * (1.0 / math.sqrt(F))


def early_kernel(tile, *refs):
    given, table, out = refs[:-2], refs[-2], refs[-1]
    for t in range(LAGS // tile):
        columns = pl.ds(t * tile, tile)
        out[:, columns] = lag_sum(given, table, columns)


def late_kernel(count, tile, *refs):
    given, table, early, out = refs[:-3], refs[-3], refs[-2], refs[-1]
    columns = pl.ds(pl.multiple_of(pl.program_id(0) * tile, tile), tile)
    both = [early[:, columns], lag_sum(given, table, columns)]
    both = [v.reshape(count, v.shape[0] // count, tile) for v in both]
    out[...] = jnp.concatenate(both, axis=1).astype(jnp.bfloat16)


def lags_early(group, table):
    arrays = [piece for half in group for piece in half]
    vmem = pl.BlockSpec(memory_space=pltpu.VMEM)
    return pl.pallas_call(
        functools.partial(early_kernel, 512),
        in_specs=[vmem] * (len(arrays) + 1),
        out_specs=vmem,
        out_shape=pltpu.VMEM((arrays[0].shape[1], LAGS), jnp.float32),
        compiler_params=pltpu.CompilerParams(vmem_limit_bytes=12 * MIB),
        cost_estimate=busy(1.5),
        name="lags_early",
    )(*arrays, table)


def lags_late(group, table, early, count, number):
    arrays = [piece for half in group for piece in half]
    vmem = pl.BlockSpec(memory_space=pltpu.VMEM)
    tile = 512
    return pl.pallas_call(
        functools.partial(late_kernel, count, tile),
        grid=(LAGS // tile,),
        in_specs=[vmem] * (len(arrays) + 2),
        out_specs=pl.BlockSpec((count, number, tile), lambda i: (0, 0, i)),
        out_shape=jax.ShapeDtypeStruct((count, number, LAGS), jnp.bfloat16),
        compiler_params=pltpu.CompilerParams(vmem_limit_bytes=16 * MIB),
        cost_estimate=busy(2.0),
        name="lags_late",
    )(*arrays, table, early)


def solution(mesh):
    ring = mesh.shape["chan"]
    if ring % TEAM:
        raise ValueError("chan")

    def swapped(value, by):
        return lax.ppermute(value, "chan", [(i, i ^ by) for i in range(ring)])

    def down(value, hops):
        pairs = [(i, i - TEAM) for i in range(TEAM, ring) if i // TEAM + hops - 1 < ring // TEAM]
        return lax.ppermute(value, "chan", pairs)

    def shards(records, live_mask, offsets):
        count, windows, length = records.shape
        span = TEAM * count
        number = offsets.shape[0]
        forward, inverse = tables(length)
        own0, own1, far0, far1 = spectra(records, live_mask, jnp.asarray(forward))
        across0, across1 = swapped(far0, 2), swapped(far1, 2)
        reach = min((span + BAND - 2) // span, ring // TEAM - 1)
        chunks = [[[own0, across0], [own1, across1]]]
        for hops in range(1, reach + 1):
            previous = chunks[-1]
            chunks.append([[down(c, hops) for c in half] for half in previous])
        planes = [
            [[piece for c in half for piece in (c, swapped(c, 1))] for half in chunk] for chunk in chunks
        ]
        parts = []
        for first, last in ((0, number // 2), (number // 2, number)):
            group = []
            for half in range(HALVES):
                near, far = cross(windows, count, first, last, offsets, [p[half] for p in planes])
                back = swapped(far, 2)
                group.append([near, swapped(near, 1), back, swapped(back, 1)])
            parts.append(group)
        inverse = jnp.asarray(inverse)
        return lags_late(parts[1], inverse, lags_early(parts[0], inverse), count, number)

    in_specs = (P(("day", "chan"), None, None), P(("day", "chan")), P())
    out_specs = P(("day", "chan"), None, None)
    return jax.shard_map(shards, mesh=mesh, in_specs=in_specs, out_specs=out_specs, check_vma=False)
```

```python
import functools
import math

import jax
import jax.numpy as jnp
import ml_dtypes
import numpy as np
from jax import lax
from jax.experimental import pallas as pl
from jax.experimental.pallas import tpu as pltpu
from jax.sharding import PartitionSpec as P

F = 512
F0 = 6
LAGS = 2048
BAND = 512
TEAM = 4
HALVES = 2
LANES = 128
BINS = F // (TEAM * HALVES)
QUADRANTS = 4

MIB = 1024 * 1024


def busy(microseconds):
    return pl.CostEstimate(flops=int(microseconds * 1.1535e9), bytes_accessed=0, transcendentals=0)


def column_order():
    kinds = np.asarray([0, 2, 1, 3])[(F0 + np.arange(F)) % QUADRANTS]
    bins = np.argsort(kinds, kind="stable").reshape(TEAM, HALVES, 1, BINS)
    parts = np.arange(2).reshape(1, 1, 2, 1) * F
    return (bins + parts).reshape(-1)


def tables(length):
    freqs = F0 + np.arange(F, dtype=np.int64)
    unit = np.float32(2.0 * math.pi / length)

    def cut(phase):
        angle = unit * np.mod(phase, length).astype(np.float32)
        return np.cos(angle), -np.sin(angle)

    order = column_order()
    part = length // QUADRANTS
    forward = np.concatenate(cut(np.arange(part)[:, None] * freqs[None, :]), axis=1)[:, order]
    forward = forward.reshape(part, 2, F).transpose(1, 0, 2)
    shifts = np.arange(LAGS, dtype=np.int64) - LAGS // 2
    inverse = np.concatenate(cut(freqs[:, None] * shifts[None, :]), axis=0)[order]
    inverse = inverse.reshape(TEAM, 2 * F // TEAM, LAGS)
    return forward.astype(ml_dtypes.bfloat16), inverse.astype(ml_dtypes.bfloat16)


def spectra_kernel(windows, records_hbm, table_hbm, live_hbm, mine, sibling, far0, far1, records, table, live, spec, scales, sems):
    rows, length = records.shape
    count = rows // windows
    part = length // QUADRANTS
    pitch = windows + 1
    pairs = [(records_hbm, records), (table_hbm.at[0], table.at[0]), (table_hbm.at[1], table.at[1]), (live_hbm, live)]
    copies = [pltpu.make_async_copy(a, b, sems.at[n]) for n, (a, b) in enumerate(pairs)]
    for copy in copies:
        copy.start()
    me = lax.rem(lax.axis_index("chan"), TEAM)
    real_lane = lax.broadcasted_iota(jnp.int32, (rows, LANES), 1) < BINS
    copies[0].wait()
    x0, x1, x2, x3 = (records[:, q * part : (q + 1) * part] for q in range(QUADRANTS))

    def both(first, second, columns):
        total = jnp.dot(first, columns, preferred_element_type=jnp.float32)
        return total + jnp.dot(second, columns, preferred_element_type=jnp.float32)

    squares = jnp.zeros((rows, LANES), jnp.float32)
    for odd in range(2):
        copies[1 + odd].wait()
        columns = table[odd]
        if odd:
            left, right = both(x0, -x2, columns), both(x1, -x3, columns)
        else:
            left, right = both(x0, x2, columns), both(x1, x3, columns)
        for c in range(2):
            for half in range(HALVES):
                at = (c * HALVES + half) * LANES
                near, other = left[:, at : at + LANES], right[:, at : at + LANES]
                if odd:
                    other = pltpu.roll(other, BINS, 1)
                    value = near + jnp.where(real_lane == (c == 0), other, -other)
                else:
                    value = near + other if c == 0 else near - other
                squares = squares + value * value
                for channel in range(count):
                    rows_of = slice(channel * windows, (channel + 1) * windows)
                    spec[(2 * odd + c) * HALVES + half, channel * pitch : channel * pitch + windows, :] = value[rows_of]
    copies[3].wait()
    channel = lax.broadcasted_iota(jnp.int32, (rows, count), 0) // windows
    lane = lax.broadcasted_iota(jnp.int32, (rows, count), 1)
    mask = jnp.where(channel == lane, live[...].astype(jnp.float32), 0.0)
    gain = jnp.sum(mask, axis=1, keepdims=True)
    power = jnp.sum(squares, axis=1, keepdims=True)
    scale = jnp.broadcast_to(gain * lax.rsqrt(power * (1.0 / (2 * F)) + 1e-06), (rows, LANES))
    for channel in range(count):
        scales[channel * pitch : channel * pitch + windows, :] = scale[channel * windows : (channel + 1) * windows]
    for w in range(windows):
        every = pl.ds(w, count, stride=pitch)
        factor = scales[every, :]
        for half, far in enumerate((far0, far1)):
            places = [mine.at[half], sibling.at[half], far.at[0], far.at[1]]
            for d, place in enumerate(places):
                quarter = jnp.bitwise_xor(me, d)
                piece = spec[quarter * HALVES + half, every, :] * factor
                place[w * count : (w + 1) * count, :] = piece.astype(jnp.bfloat16)


def spectra(records, live_mask, table):
    count, windows, length = records.shape
    rows = count * windows
    return pl.pallas_call(
        functools.partial(spectra_kernel, windows),
        in_specs=[
            pl.BlockSpec(memory_space=pl.ANY),
            pl.BlockSpec(memory_space=pl.ANY),
            pl.BlockSpec(memory_space=pl.ANY),
        ],
        out_specs=[pl.BlockSpec(memory_space=pltpu.VMEM)] * 4,
        out_shape=[pltpu.VMEM((2, rows, LANES), jnp.bfloat16)] * 4,
        scratch_shapes=[
            pltpu.VMEM((rows, length), jnp.bfloat16),
            pltpu.VMEM(table.shape, jnp.bfloat16),
            pltpu.VMEM((1, count), jnp.int32),
            pltpu.VMEM((TEAM * HALVES, count * (windows + 1), LANES), jnp.float32),
            pltpu.VMEM((count * (windows + 1), LANES), jnp.float32),
            pltpu.SemaphoreType.DMA((4,)),
        ],
        compiler_params=pltpu.CompilerParams(vmem_limit_bytes=58 * MIB),
        cost_estimate=busy(3.0),
        name="spectra",
    )(records.reshape(rows, length), table, live_mask.reshape(1, count))


def join_kernel(first, second, out):
    for half in range(out.shape[0] // 2):
        out[2 * half] = first[half]
        out[2 * half + 1] = second[half]


def joined(first, second):
    vmem = pl.BlockSpec(memory_space=pltpu.VMEM)
    return pl.pallas_call(
        join_kernel,
        in_specs=[vmem] * 2,
        out_specs=vmem,
        out_shape=pltpu.VMEM((2 * first.shape[0],) + first.shape[1:], first.dtype),
        compiler_params=pltpu.CompilerParams(vmem_limit_bytes=2 * MIB),
        cost_estimate=busy(0.3),
        name="joined",
    )(first, second)


def far_kernel(straight, crossed, out):
    out[0] = straight[0]
    out[1] = crossed[1]


def far_joined(straight, crossed):
    vmem = pl.BlockSpec(memory_space=pltpu.VMEM)
    return pl.pallas_call(
        far_kernel,
        in_specs=[vmem] * 2,
        out_specs=vmem,
        out_shape=pltpu.VMEM(straight.shape, straight.dtype),
        compiler_params=pltpu.CompilerParams(vmem_limit_bytes=2 * MIB),
        cost_estimate=busy(0.3),
        name="far_joined",
    )(straight, crossed)


def cross_kernel(windows, count, halves, first, last, low, planes, offsets, *refs):
    each = 1 + len(halves)
    given, (near, far, side, extended, paired) = refs[: each * (planes + 1)], refs[each * (planes + 1) :]
    me = lax.rem(lax.axis_index("chan"), TEAM)
    span = TEAM * count
    number = last - first
    pitch = number + 1
    blocks = [jnp.bitwise_xor(me, d) for d in range(TEAM)]
    lane = lax.broadcasted_iota(jnp.int32, (8, LANES), 1)
    real_lane = lane < BINS
    sign = jnp.where(real_lane, 1.0 / windows, -1.0 / windows)
    tail = extended.shape[1] - planes * span
    if tail:
        extended[:, planes * span :, :] = jnp.zeros((windows, tail, LANES), jnp.float32)

    for n, half in enumerate(halves):

        def pieces(plane):
            own, across = given[each * plane], given[each * plane + 1 + n]
            return own.at[2 * half], own.at[2 * half + 1], across.at[0], across.at[1]

        for d, ref in enumerate(pieces(0)):
            for w in range(windows):
                side[w, d * count : (d + 1) * count, :] = ref[w * count : (w + 1) * count, :].astype(jnp.float32)
        for plane in range(planes):
            for d, ref in enumerate(pieces(plane + 1)):
                start = pl.multiple_of(plane * span + blocks[d] * count, count)
                for w in range(windows):
                    extended[w, pl.ds(start, count), :] = ref[w * count : (w + 1) * count, :].astype(jnp.float32)

        def group(step, carry):
            at = pl.multiple_of(step * 8, 8)
            d = step // (count // 8)
            within = lax.rem(step, count // 8) * 8
            channel = jnp.bitwise_xor(me, d) * count + within
            straight, turned = [], []
            for w in range(windows):
                value = side[w, pl.ds(at, 8), :]
                straight.append(value * (1.0 / windows))
                turned.append(pltpu.roll(value, BINS, 1) * sign)
            for j in range(number):
                place = channel + offsets[first + j] - low * span
                real_part, imag_part = None, None
                for w in range(windows):
                    partner = extended[w, pl.ds(place, 8), :]
                    r, i = straight[w] * partner, turned[w] * partner
                    real_part = r if w == 0 else real_part + r
                    imag_part = i if w == 0 else imag_part + i
                folded = pltpu.roll(jnp.where(real_lane, imag_part, real_part), BINS, 1)
                both = jnp.where(real_lane, real_part, imag_part) + folded
                paired[d, pl.ds(within * pitch + j, 8, stride=pitch), :] = both
            return carry

        lax.fori_loop(0, span // 8, group, 0, unroll=2)
        for d in range(TEAM):
            out = (near if d < 2 else far).at[2 * n + d % 2]
            for k in range(0, count, 2):
                rows = [paired[d, (k + m) * pitch : (k + m) * pitch + number, :] for m in range(2)]
                out[k * number : (k + 2) * number, :] = jnp.concatenate(rows, axis=0).astype(jnp.bfloat16)


def cross(windows, count, halves, first, last, offsets, team_planes):
    span = TEAM * count
    stride = BAND // offsets.shape[0]
    low = (first * stride + 1) // span
    high = (span - 1 + last * stride) // span
    planes = [team_planes[0]] + [team_planes[p] for p in range(low, min(high, len(team_planes) - 1) + 1)]
    given = [c for plane in planes for c in [plane[0]] + [plane[1 + half] for half in halves]]
    number = last - first
    vmem = pl.BlockSpec(memory_space=pltpu.VMEM)
    return pl.pallas_call(
        functools.partial(cross_kernel, windows, count, halves, first, last, low, len(planes) - 1),
        in_specs=[pl.BlockSpec(memory_space=pltpu.SMEM)] + [vmem] * len(given),
        out_specs=[vmem] * 2,
        out_shape=[pltpu.VMEM((2 * len(halves), count * number, LANES), jnp.bfloat16)] * 2,
        scratch_shapes=[
            pltpu.VMEM((windows, span, LANES), jnp.float32),
            pltpu.VMEM((windows, (high - low + 1) * span, LANES), jnp.float32),
            pltpu.VMEM((TEAM, count * (number + 1), LANES), jnp.float32),
        ],
        compiler_params=pltpu.CompilerParams(vmem_limit_bytes=8 * MIB),
        cost_estimate=busy(2.0 * len(halves)),
        name="cross",
    )(offsets, *given)


def lag_sum(given, table, columns):
    me = lax.rem(lax.axis_index("chan"), TEAM)
    total = None
    for d in range(TEAM):
        left = jnp.concatenate([given[h * TEAM + d] for h in range(HALVES)], axis=1)
        term = jnp.dot(left, table[jnp.bitwise_xor(me, d), :, columns], preferred_element_type=jnp.float32)
        total = term if d == 0 else total + term
    return total * (1.0 / math.sqrt(F))


def picked(refs, picks):
    return [refs[n][at] for n, at in picks]


def early_kernel(tile, picks, *refs):
    given, table, out = picked(refs, picks), refs[-2], refs[-1]
    for t in range(LAGS // tile):
        columns = pl.ds(t * tile, tile)
        out[:, columns] = lag_sum(given, table, columns)


def late_kernel(count, tile, picks, *refs):
    given, table, early, out = picked(refs, picks), refs[-3], refs[-2], refs[-1]
    columns = pl.ds(pl.multiple_of(pl.program_id(0) * tile, tile), tile)
    both = [early[:, columns], lag_sum(given, table, columns)]
    both = [v.reshape(count, v.shape[0] // count, tile) for v in both]
    out[...] = jnp.concatenate(both, axis=1).astype(jnp.bfloat16)


def lags_early(arrays, picks, table):
    vmem = pl.BlockSpec(memory_space=pltpu.VMEM)
    return pl.pallas_call(
        functools.partial(early_kernel, 512, picks),
        in_specs=[vmem] * (len(arrays) + 1),
        out_specs=vmem,
        out_shape=pltpu.VMEM((arrays[0].shape[1], LAGS), jnp.float32),
        compiler_params=pltpu.CompilerParams(vmem_limit_bytes=12 * MIB),
        cost_estimate=busy(1.5),
        name="lags_early",
    )(*arrays, table)


def lags_late(arrays, picks, table, early, count, number):
    vmem = pl.BlockSpec(memory_space=pltpu.VMEM)
    tile = 512
    return pl.pallas_call(
        functools.partial(late_kernel, count, tile, picks),
        grid=(LAGS // tile,),
        in_specs=[vmem] * (len(arrays) + 2),
        out_specs=pl.BlockSpec((count, number, tile), lambda i: (0, 0, i)),
        out_shape=jax.ShapeDtypeStruct((count, number, LAGS), jnp.bfloat16),
        compiler_params=pltpu.CompilerParams(vmem_limit_bytes=16 * MIB),
        cost_estimate=busy(2.0),
        name="lags_late",
    )(*arrays, table, early)


def solution(mesh):
    ring = mesh.shape["chan"]
    if ring % TEAM:
        raise ValueError("chan")

    def swapped(value, by):
        return lax.ppermute(value, "chan", [(i, i ^ by) for i in range(ring)])

    def down(value, hops):
        pairs = [(i, i - TEAM) for i in range(TEAM, ring) if i // TEAM + hops - 1 < ring // TEAM]
        return lax.ppermute(value, "chan", pairs)

    def shards(records, live_mask, offsets):
        count, windows, length = records.shape
        span = TEAM * count
        number = offsets.shape[0]
        forward, inverse = tables(length)
        mine, sibling, far0, far1 = spectra(records, live_mask, jnp.asarray(forward))
        inverse = jnp.asarray(inverse)
        near = joined(mine, swapped(sibling, 1))
        across = [swapped(far, 2) for far in (far0, far1)]
        chunks = [[near] + [far_joined(c, swapped(c, 1)) for c in across]]
        reach = min((span + BAND - 2) // span, ring // TEAM - 1)
        for hops in range(1, reach + 1):
            chunks.append([down(c, hops) for c in chunks[-1]])

        def returned(halves, first, last):
            near, far = cross(windows, count, halves, first, last, offsets, chunks)
            back = swapped(far, 2)
            arrays = [near, swapped(near, 1), back, swapped(back, 1)]
            return arrays, [(d, 2 * n + d % 2) for n in range(len(halves)) for d in range(TEAM)]

        middle = number // 2
        arrays, picks = returned((0, 1), 0, middle)
        early = lags_early(arrays, picks, inverse)
        arrays, picks = returned((0,), middle, number)
        more, rest = returned((1,), middle, number)
        picks = picks + [(len(arrays) + n, at) for n, at in rest]
        return lags_late(arrays + more, picks, inverse, early, count, number)

    in_specs = (P(("day", "chan"), None, None), P(("day", "chan")), P())
    out_specs = P(("day", "chan"), None, None)
    return jax.shard_map(shards, mesh=mesh, in_specs=in_specs, out_specs=out_specs, check_vma=False)
```

```python
import functools
import math

import jax
import jax.numpy as jnp
import ml_dtypes
import numpy as np
from jax import lax
from jax.experimental import pallas as pl
from jax.experimental.pallas import tpu as pltpu
from jax.sharding import PartitionSpec as P

F = 512
F0 = 6
LAGS = 2048
BAND = 512
TEAM = 4
HALVES = 2
LANES = 128
BINS = F // (TEAM * HALVES)
QUADRANTS = 4

MIB = 1024 * 1024
JOIN = 2


def busy(microseconds):
    return pl.CostEstimate(flops=int(microseconds * 1.1535e9), bytes_accessed=0, transcendentals=0)


def column_order():
    kinds = np.asarray([0, 2, 1, 3])[(F0 + np.arange(F)) % QUADRANTS]
    bins = np.argsort(kinds, kind="stable").reshape(TEAM, HALVES, 1, BINS)
    parts = np.arange(2).reshape(1, 1, 2, 1) * F
    return (bins + parts).reshape(-1)


def tables(length):
    freqs = F0 + np.arange(F, dtype=np.int64)
    unit = np.float32(2.0 * math.pi / length)

    def cut(phase):
        angle = unit * np.mod(phase, length).astype(np.float32)
        return np.cos(angle), -np.sin(angle)

    order = column_order()
    part = length // QUADRANTS
    forward = np.concatenate(cut(np.arange(part)[:, None] * freqs[None, :]), axis=1)[:, order]
    forward = forward.reshape(part, 2, F).transpose(1, 0, 2)
    shifts = np.arange(LAGS, dtype=np.int64) - LAGS // 2
    inverse = np.concatenate(cut(freqs[:, None] * shifts[None, :]), axis=0)[order]
    inverse = inverse.reshape(TEAM, HALVES, LANES, LAGS).transpose(1, 0, 2, 3).reshape(HALVES, TEAM // 2, 2 * LANES, LAGS)
    return forward.astype(ml_dtypes.bfloat16), inverse.astype(ml_dtypes.bfloat16)


def spectra_kernel(windows, records_hbm, table_hbm, live_hbm, mine, sibling, far0, far1, records, table, live, spec, scales, sems):
    rows, length = records.shape
    count = rows // windows
    part = length // QUADRANTS
    pitch = windows + 1
    pairs = [(records_hbm, records), (table_hbm.at[0], table.at[0]), (table_hbm.at[1], table.at[1]), (live_hbm, live)]
    copies = [pltpu.make_async_copy(a, b, sems.at[n]) for n, (a, b) in enumerate(pairs)]
    for copy in copies:
        copy.start()
    me = lax.rem(lax.axis_index("chan"), TEAM)
    real_lane = lax.broadcasted_iota(jnp.int32, (rows, LANES), 1) < BINS
    copies[0].wait()
    x0, x1, x2, x3 = (records[:, q * part : (q + 1) * part] for q in range(QUADRANTS))

    def both(first, second, columns):
        total = jnp.dot(first, columns, preferred_element_type=jnp.float32)
        return total + jnp.dot(second, columns, preferred_element_type=jnp.float32)

    squares = jnp.zeros((rows, LANES), jnp.float32)
    for odd in range(2):
        copies[1 + odd].wait()
        columns = table[odd]
        if odd:
            left, right = both(x0, -x2, columns), both(x1, -x3, columns)
        else:
            left, right = both(x0, x2, columns), both(x1, x3, columns)
        for c in range(2):
            for half in range(HALVES):
                at = (c * HALVES + half) * LANES
                near, other = left[:, at : at + LANES], right[:, at : at + LANES]
                if odd:
                    other = pltpu.roll(other, BINS, 1)
                    value = near + jnp.where(real_lane == (c == 0), other, -other)
                else:
                    value = near + other if c == 0 else near - other
                squares = squares + value * value
                for channel in range(count):
                    rows_of = slice(channel * windows, (channel + 1) * windows)
                    spec[(2 * odd + c) * HALVES + half, channel * pitch : channel * pitch + windows, :] = value[rows_of]
    copies[3].wait()
    channel = lax.broadcasted_iota(jnp.int32, (rows, count), 0) // windows
    lane = lax.broadcasted_iota(jnp.int32, (rows, count), 1)
    mask = jnp.where(channel == lane, live[...].astype(jnp.float32), 0.0)
    gain = jnp.sum(mask, axis=1, keepdims=True)
    power = jnp.sum(squares, axis=1, keepdims=True)
    scale = jnp.broadcast_to(gain * lax.rsqrt(power * (1.0 / (2 * F)) + 1e-06), (rows, LANES))
    for channel in range(count):
        scales[channel * pitch : channel * pitch + windows, :] = scale[channel * windows : (channel + 1) * windows]
    for w in range(windows):
        every = pl.ds(w, count, stride=pitch)
        factor = scales[every, :]
        for half, far in enumerate((far0, far1)):
            places = [mine.at[half], sibling.at[half], far.at[0], far.at[1]]
            for d, place in enumerate(places):
                quarter = jnp.bitwise_xor(me, d)
                piece = spec[quarter * HALVES + half, every, :] * factor
                place[w * count : (w + 1) * count, :] = piece.astype(jnp.bfloat16)


def spectra(records, live_mask, table):
    count, windows, length = records.shape
    rows = count * windows
    return pl.pallas_call(
        functools.partial(spectra_kernel, windows),
        in_specs=[
            pl.BlockSpec(memory_space=pl.ANY),
            pl.BlockSpec(memory_space=pl.ANY),
            pl.BlockSpec(memory_space=pl.ANY),
        ],
        out_specs=[pl.BlockSpec(memory_space=pltpu.VMEM)] * 4,
        out_shape=[pltpu.VMEM((2, rows, LANES), jnp.bfloat16)] * 4,
        scratch_shapes=[
            pltpu.VMEM((rows, length), jnp.bfloat16),
            pltpu.VMEM(table.shape, jnp.bfloat16),
            pltpu.VMEM((1, count), jnp.int32),
            pltpu.VMEM((TEAM * HALVES, count * (windows + 1), LANES), jnp.float32),
            pltpu.VMEM((count * (windows + 1), LANES), jnp.float32),
            pltpu.SemaphoreType.DMA((4,)),
        ],
        compiler_params=pltpu.CompilerParams(vmem_limit_bytes=58 * MIB),
        cost_estimate=busy(3.0),
        name="spectra",
    )(records.reshape(rows, length), table, live_mask.reshape(1, count))


def join_kernel(first, second, out):
    for half in range(out.shape[0] // 2):
        out[2 * half] = first[half]
        out[2 * half + 1] = second[half]


def joined(first, second):
    vmem = pl.BlockSpec(memory_space=pltpu.VMEM)
    return pl.pallas_call(
        join_kernel,
        in_specs=[vmem] * 2,
        out_specs=vmem,
        out_shape=pltpu.VMEM((2 * first.shape[0],) + first.shape[1:], first.dtype),
        compiler_params=pltpu.CompilerParams(vmem_limit_bytes=2 * MIB),
        cost_estimate=busy(0.3),
        name="joined",
    )(first, second)


def team_kernel(half, near, far, out):
    for d in range(2):
        out[d] = near[2 * half + d]
        out[2 + d] = far[d]


def team_joined(half, near, far):
    vmem = pl.BlockSpec(memory_space=pltpu.VMEM)
    return pl.pallas_call(
        functools.partial(team_kernel, half),
        in_specs=[vmem] * 2,
        out_specs=vmem,
        out_shape=pltpu.VMEM((TEAM,) + far.shape[1:], far.dtype),
        compiler_params=pltpu.CompilerParams(vmem_limit_bytes=2 * MIB),
        cost_estimate=busy(0.3),
        name="team_joined",
    )(near, far)


def far_kernel(straight, crossed, out):
    out[0] = straight[0]
    out[1] = crossed[1]


def far_joined(straight, crossed):
    vmem = pl.BlockSpec(memory_space=pltpu.VMEM)
    return pl.pallas_call(
        far_kernel,
        in_specs=[vmem] * 2,
        out_specs=vmem,
        out_shape=pltpu.VMEM(straight.shape, straight.dtype),
        compiler_params=pltpu.CompilerParams(vmem_limit_bytes=2 * MIB),
        cost_estimate=busy(0.3),
        name="far_joined",
    )(straight, crossed)


def cross_kernel(windows, count, halves, sizes, first, last, low, planes, offsets, *refs):
    near, far, side, extended, paired = refs[-5:]
    given = list(refs[:-5])
    pieces = []
    for size in sizes:
        arrays, given = given[:size], given[size:]
        if size == len(halves):
            pieces.append([[a.at[d] for d in range(TEAM)] for a in arrays])
        else:
            pieces.append([[arrays[0].at[2 * h + d] for d in range(2)] + [a.at[d] for d in range(2)] for h, a in zip(halves, arrays[1:])])
    me = lax.rem(lax.axis_index("chan"), TEAM)
    span = TEAM * count
    number = last - first
    pitch = number + 1
    blocks = [jnp.bitwise_xor(me, d) for d in range(TEAM)]
    lane = lax.broadcasted_iota(jnp.int32, (8, LANES), 1)
    real_lane = lane < BINS
    sign = jnp.where(real_lane, 1.0 / windows, -1.0 / windows)
    tail = extended.shape[1] - planes * span
    if tail:
        extended[:, planes * span :, :] = jnp.zeros((windows, tail, LANES), jnp.float32)

    for n in range(len(halves)):
        for d, ref in enumerate(pieces[0][n]):
            for w in range(windows):
                side[w, d * count : (d + 1) * count, :] = ref[w * count : (w + 1) * count, :].astype(jnp.float32)
        for plane in range(planes):
            for d, ref in enumerate(pieces[len(sizes) - planes + plane][n]):
                start = pl.multiple_of(plane * span + blocks[d] * count, count)
                for w in range(windows):
                    extended[w, pl.ds(start, count), :] = ref[w * count : (w + 1) * count, :].astype(jnp.float32)

        def group(step, carry):
            at = pl.multiple_of(step * 8, 8)
            d = step // (count // 8)
            within = lax.rem(step, count // 8) * 8
            channel = jnp.bitwise_xor(me, d) * count + within
            straight, turned = [], []
            for w in range(windows):
                value = side[w, pl.ds(at, 8), :]
                straight.append(value * (1.0 / windows))
                turned.append(pltpu.roll(value, BINS, 1) * sign)
            for j in range(number):
                place = channel + offsets[first + j] - low * span
                real_part, imag_part = None, None
                for w in range(windows):
                    partner = extended[w, pl.ds(place, 8), :]
                    r, i = straight[w] * partner, turned[w] * partner
                    real_part = r if w == 0 else real_part + r
                    imag_part = i if w == 0 else imag_part + i
                folded = pltpu.roll(jnp.where(real_lane, imag_part, real_part), BINS, 1)
                both = jnp.where(real_lane, real_part, imag_part) + folded
                paired[d, pl.ds(within * pitch + j, 8, stride=pitch), :] = both
            return carry

        lax.fori_loop(0, span // 8, group, 0, unroll=True)
        for d in range(TEAM):
            out = (near if d < 2 else far).at[2 * n + d % 2]
            for k in range(0, count, 2):
                rows = [paired[d, (k + m) * pitch : (k + m) * pitch + number, :] for m in range(2)]
                out[k * number : (k + 2) * number, :] = jnp.concatenate(rows, axis=0).astype(jnp.bfloat16)


def cross(windows, count, halves, first, last, offsets, team_planes):
    span = TEAM * count
    stride = BAND // offsets.shape[0]
    low = (first * stride + 1) // span
    high = (span - 1 + last * stride) // span
    top = min(high, len(team_planes) - 1)
    used = [0] * (low > 0) + list(range(low, top + 1))
    groups = []
    for plane in (team_planes[p] for p in used):
        split = len(plane) > HALVES
        groups.append([plane[0]] * split + [plane[split + half] for half in halves])
    sizes = tuple(len(g) for g in groups)
    given = [c for g in groups for c in g]
    number = last - first
    vmem = pl.BlockSpec(memory_space=pltpu.VMEM)
    return pl.pallas_call(
        functools.partial(cross_kernel, windows, count, halves, sizes, first, last, low, top - low + 1),
        in_specs=[pl.BlockSpec(memory_space=pltpu.SMEM)] + [vmem] * len(given),
        out_specs=[vmem] * 2,
        out_shape=[pltpu.VMEM((2 * len(halves), count * number, LANES), jnp.bfloat16)] * 2,
        scratch_shapes=[
            pltpu.VMEM((windows, span, LANES), jnp.float32),
            pltpu.VMEM((windows, (high - low + 1) * span, LANES), jnp.float32),
            pltpu.VMEM((TEAM, count * (number + 1), LANES), jnp.float32),
        ],
        compiler_params=pltpu.CompilerParams(vmem_limit_bytes=8 * MIB),
        cost_estimate=busy(0.5 * len(halves)),
        name="cross",
    )(offsets, *given)


def lag_sum(pieces, table, half, columns):
    me = lax.rem(lax.axis_index("chan"), TEAM)
    odd = lax.rem(me, 2) == 1
    total = None
    for chip in range(TEAM // 2):
        first, second = pieces[2 * chip], pieces[2 * chip + 1]
        left = jnp.concatenate([jnp.where(odd, second, first), jnp.where(odd, first, second)], axis=1)
        right = table[half, jnp.bitwise_xor(me // 2, chip), :, columns]
        term = jnp.dot(left, right, preferred_element_type=jnp.float32)
        total = term if chip == 0 else total + term
    return total * (1.0 / math.sqrt(F))


def early_kernel(tile, *refs):
    low, high, (table, lower, upper) = refs[: HALVES * TEAM], refs[HALVES * TEAM : -3], refs[-3:]
    for t in range(LAGS // tile):
        columns = pl.ds(t * tile, tile)
        shares = [lag_sum([low[h * TEAM + d][d % 2] for d in range(TEAM)], table, h, columns) for h in range(HALVES)]
        lower[:, columns] = shares[0] + shares[1]
        upper[:, columns] = lag_sum([high[d][d % 2] for d in range(TEAM)], table, 0, columns)


def late_kernel(count, tile, *refs):
    high, table, lower, upper, out = refs[:TEAM], refs[-4], refs[-3], refs[-2], refs[-1]
    columns = pl.ds(pl.multiple_of(pl.program_id(0) * tile, tile), tile)
    rest = lag_sum([high[d][d % 2] for d in range(TEAM)], table, 1, columns)
    both = [lower[:, columns], upper[:, columns] + rest]
    both = [v.reshape(count, v.shape[0] // count, tile) for v in both]
    out[...] = jnp.concatenate(both, axis=1).astype(jnp.bfloat16)


def lags_early(low, high, table):
    vmem = pl.BlockSpec(memory_space=pltpu.VMEM)
    return pl.pallas_call(
        functools.partial(early_kernel, 512),
        in_specs=[vmem] * (len(low) + len(high) + 1),
        out_specs=[vmem] * 2,
        out_shape=[pltpu.VMEM((v[0].shape[1], LAGS), jnp.float32) for v in (low, high)],
        compiler_params=pltpu.CompilerParams(vmem_limit_bytes=12 * MIB),
        cost_estimate=busy(0.1),
        name="lags_early",
    )(*low, *high, table)


def lags_late(high, table, lower, upper, count, number):
    vmem = pl.BlockSpec(memory_space=pltpu.VMEM)
    tile = 1024
    return pl.pallas_call(
        functools.partial(late_kernel, count, tile),
        grid=(LAGS // tile,),
        in_specs=[vmem] * (TEAM + 3),
        out_specs=pl.BlockSpec((count, number, tile), lambda i: (0, 0, i)),
        out_shape=jax.ShapeDtypeStruct((count, number, LAGS), jnp.bfloat16),
        compiler_params=pltpu.CompilerParams(vmem_limit_bytes=16 * MIB),
        cost_estimate=busy(2.0),
        name="lags_late",
    )(*high, table, lower, upper)


def solution(mesh):
    ring = mesh.shape["chan"]
    if ring % TEAM:
        raise ValueError("chan")

    def after(value, *others):
        return lax.optimization_barrier((value,) + others)[0] if others else value

    def swapped(value, by):
        return lax.ppermute(value, "chan", [(i, i ^ by) for i in range(ring)])

    def down(value, hops):
        pairs = [(i, i - TEAM) for i in range(TEAM, ring) if i // TEAM + hops - 1 < ring // TEAM]
        return lax.ppermute(value, "chan", pairs)

    def shards(records, live_mask, offsets):
        count, windows, length = records.shape
        span = TEAM * count
        number = offsets.shape[0]
        forward, inverse = tables(length)
        mine, sibling, far0, far1 = spectra(records, live_mask, jnp.asarray(forward))
        inverse = jnp.asarray(inverse)
        near = joined(mine, swapped(sibling, 1))
        across = [swapped(far, 2) for far in (far0, far1)]
        own = [near] + [far_joined(c, swapped(c, 1)) for c in across]
        reach = min((span + BAND - 2) // span, ring // TEAM - 1)
        middle = number // 2

        def crossed(halves, first, last, planes, others=(), before=()):
            planes = [[after(planes[0][0], *others)] + planes[0][1:]] + planes[1:]
            near, far = cross(windows, count, halves, first, last, offsets, planes)
            return near, swapped(after(far, *before), 2)

        def gathered(near, back, *others):
            return near, swapped(near, 1), back, swapped(after(back, *others), 1)

        chunks = [own]
        low = []
        for hops in range(1, reach + 1):
            arrived = [down(c, hops) for c in chunks[-1]]
            if hops == JOIN:
                first = team_joined(0, arrived[0], arrived[1])
                low = [crossed((0,), 0, middle, chunks + [[first, None]])]
                arrived = [first, team_joined(1, arrived[0], after(arrived[2], low[0][0]))]
            chunks.append(arrived)
        for half in range(len(low), HALVES):
            low.append(crossed((half,), 0, middle, chunks))
        near0, back0 = crossed((0,), middle, number, chunks)
        near1, back1 = crossed((1,), middle, number, chunks)
        low = gathered(*low[0], near1) + gathered(*low[1], near1)
        high = gathered(near0, back0, near1)
        lower, upper = lags_early(low, high, inverse)
        rest = gathered(near1, back1, lower)
        return lags_late(rest, inverse, lower, upper, count, number)

    in_specs = (P(("day", "chan"), None, None), P(("day", "chan")), P())
    out_specs = P(("day", "chan"), None, None)
    return jax.shard_map(shards, mesh=mesh, in_specs=in_specs, out_specs=out_specs, check_vma=False)
```

```python
import functools
import math

import jax
import jax.numpy as jnp
import ml_dtypes
import numpy as np
from jax import lax
from jax.experimental import pallas as pl
from jax.experimental.pallas import tpu as pltpu
from jax.sharding import PartitionSpec as P

F = 512
F0 = 6
LAGS = 2048
BAND = 512
TEAM = 4
HALVES = 2
LANES = 128
BINS = F // (TEAM * HALVES)
QUADRANTS = 4

MIB = 1024 * 1024
JOIN = 2


def busy(microseconds):
    return pl.CostEstimate(flops=int(microseconds * 1.1535e9), bytes_accessed=0, transcendentals=0)


def column_order():
    kinds = np.asarray([0, 2, 1, 3])[(F0 + np.arange(F)) % QUADRANTS]
    bins = np.argsort(kinds, kind="stable").reshape(TEAM, HALVES, 1, BINS)
    parts = np.arange(2).reshape(1, 1, 2, 1) * F
    return (bins + parts).reshape(-1)


def tables(length):
    freqs = F0 + np.arange(F, dtype=np.int64)
    unit = np.float32(2.0 * math.pi / length)

    def cut(phase):
        angle = unit * np.mod(phase, length).astype(np.float32)
        return np.cos(angle), -np.sin(angle)

    order = column_order()
    part = length // QUADRANTS
    forward = np.concatenate(cut(np.arange(part)[:, None] * freqs[None, :]), axis=1)[:, order]
    forward = forward.reshape(part, 2, F).transpose(1, 0, 2)
    shifts = np.arange(LAGS, dtype=np.int64) - LAGS // 2
    inverse = np.concatenate(cut(freqs[:, None] * shifts[None, :]), axis=0)[order]
    inverse = inverse.reshape(TEAM, HALVES, LANES, LAGS).transpose(1, 0, 2, 3).reshape(HALVES, TEAM // 2, 2 * LANES, LAGS)
    return forward.astype(ml_dtypes.bfloat16), inverse.astype(ml_dtypes.bfloat16)


def spectra_kernel(windows, records_hbm, table_hbm, live_hbm, mine, sibling, far0, far1, records, table, live, spec, scales, sems):
    rows, length = records.shape
    count = rows // windows
    part = length // QUADRANTS
    pitch = windows + 1
    pairs = [(records_hbm, records), (table_hbm.at[0], table.at[0]), (table_hbm.at[1], table.at[1]), (live_hbm, live)]
    copies = [pltpu.make_async_copy(a, b, sems.at[n]) for n, (a, b) in enumerate(pairs)]
    for copy in copies:
        copy.start()
    me = lax.rem(lax.axis_index("chan"), TEAM)
    real_lane = lax.broadcasted_iota(jnp.int32, (rows, LANES), 1) < BINS
    copies[0].wait()
    x0, x1, x2, x3 = (records[:, q * part : (q + 1) * part] for q in range(QUADRANTS))

    def both(first, second, columns):
        total = jnp.dot(first, columns, preferred_element_type=jnp.float32)
        return total + jnp.dot(second, columns, preferred_element_type=jnp.float32)

    squares = jnp.zeros((rows, LANES), jnp.float32)
    for odd in range(2):
        copies[1 + odd].wait()
        columns = table[odd]
        if odd:
            left, right = both(x0, -x2, columns), both(x1, -x3, columns)
        else:
            left, right = both(x0, x2, columns), both(x1, x3, columns)
        for c in range(2):
            for half in range(HALVES):
                at = (c * HALVES + half) * LANES
                near, other = left[:, at : at + LANES], right[:, at : at + LANES]
                if odd:
                    other = pltpu.roll(other, BINS, 1)
                    value = near + jnp.where(real_lane == (c == 0), other, -other)
                else:
                    value = near + other if c == 0 else near - other
                squares = squares + value * value
                for channel in range(count):
                    rows_of = slice(channel * windows, (channel + 1) * windows)
                    spec[(2 * odd + c) * HALVES + half, channel * pitch : channel * pitch + windows, :] = value[rows_of]
    copies[3].wait()
    channel = lax.broadcasted_iota(jnp.int32, (rows, count), 0) // windows
    lane = lax.broadcasted_iota(jnp.int32, (rows, count), 1)
    mask = jnp.where(channel == lane, live[...].astype(jnp.float32), 0.0)
    gain = jnp.sum(mask, axis=1, keepdims=True)
    power = jnp.sum(squares, axis=1, keepdims=True)
    scale = jnp.broadcast_to(gain * lax.rsqrt(power * (1.0 / (2 * F)) + 1e-06), (rows, LANES))
    for channel in range(count):
        scales[channel * pitch : channel * pitch + windows, :] = scale[channel * windows : (channel + 1) * windows]
    for w in range(windows):
        every = pl.ds(w, count, stride=pitch)
        factor = scales[every, :]
        for half, far in enumerate((far0, far1)):
            places = [mine.at[half], sibling.at[half], far.at[0], far.at[1]]
            for d, place in enumerate(places):
                quarter = jnp.bitwise_xor(me, d)
                piece = spec[quarter * HALVES + half, every, :] * factor
                place[w * count : (w + 1) * count, :] = piece.astype(jnp.bfloat16)


def spectra(records, live_mask, table):
    count, windows, length = records.shape
    rows = count * windows
    return pl.pallas_call(
        functools.partial(spectra_kernel, windows),
        in_specs=[
            pl.BlockSpec(memory_space=pl.ANY),
            pl.BlockSpec(memory_space=pl.ANY),
            pl.BlockSpec(memory_space=pl.ANY),
        ],
        out_specs=[pl.BlockSpec(memory_space=pltpu.VMEM)] * 4,
        out_shape=[pltpu.VMEM((2, rows, LANES), jnp.bfloat16)] * 4,
        scratch_shapes=[
            pltpu.VMEM((rows, length), jnp.bfloat16),
            pltpu.VMEM(table.shape, jnp.bfloat16),
            pltpu.VMEM((1, count), jnp.int32),
            pltpu.VMEM((TEAM * HALVES, count * (windows + 1), LANES), jnp.float32),
            pltpu.VMEM((count * (windows + 1), LANES), jnp.float32),
            pltpu.SemaphoreType.DMA((4,)),
        ],
        compiler_params=pltpu.CompilerParams(vmem_limit_bytes=58 * MIB),
        cost_estimate=busy(3.0),
        name="spectra",
    )(records.reshape(rows, length), table, live_mask.reshape(1, count))


def join_kernel(first, second, out):
    for half in range(out.shape[0] // 2):
        out[2 * half] = first[half]
        out[2 * half + 1] = second[half]


def joined(first, second):
    vmem = pl.BlockSpec(memory_space=pltpu.VMEM)
    return pl.pallas_call(
        join_kernel,
        in_specs=[vmem] * 2,
        out_specs=vmem,
        out_shape=pltpu.VMEM((2 * first.shape[0],) + first.shape[1:], first.dtype),
        compiler_params=pltpu.CompilerParams(vmem_limit_bytes=2 * MIB),
        cost_estimate=busy(0.3),
        name="joined",
    )(first, second)


def team_kernel(half, near, far, out):
    for d in range(2):
        out[d] = near[2 * half + d]
        out[2 + d] = far[d]


def team_joined(half, near, far):
    vmem = pl.BlockSpec(memory_space=pltpu.VMEM)
    return pl.pallas_call(
        functools.partial(team_kernel, half),
        in_specs=[vmem] * 2,
        out_specs=vmem,
        out_shape=pltpu.VMEM((TEAM,) + far.shape[1:], far.dtype),
        compiler_params=pltpu.CompilerParams(vmem_limit_bytes=2 * MIB),
        cost_estimate=busy(0.3),
        name="team_joined",
    )(near, far)


def far_kernel(straight, crossed, out):
    out[0] = straight[0]
    out[1] = crossed[1]


def far_joined(straight, crossed):
    vmem = pl.BlockSpec(memory_space=pltpu.VMEM)
    return pl.pallas_call(
        far_kernel,
        in_specs=[vmem] * 2,
        out_specs=vmem,
        out_shape=pltpu.VMEM(straight.shape, straight.dtype),
        compiler_params=pltpu.CompilerParams(vmem_limit_bytes=2 * MIB),
        cost_estimate=busy(0.3),
        name="far_joined",
    )(straight, crossed)


def cross_kernel(windows, count, halves, sizes, first, last, low, planes, apart, offsets, *refs):
    outs, (side, extended, paired) = refs[-5 - apart : -3], refs[-3:]
    given = list(refs[: -5 - apart])
    pieces = []
    for size in sizes:
        arrays, given = given[:size], given[size:]
        if size == len(halves):
            pieces.append([[a.at[d] for d in range(TEAM)] for a in arrays])
        else:
            pieces.append([[arrays[0].at[2 * h + d] for d in range(2)] + [a.at[d] for d in range(2)] for h, a in zip(halves, arrays[1:])])
    me = lax.rem(lax.axis_index("chan"), TEAM)
    span = TEAM * count
    number = last - first
    pitch = number + 1
    blocks = [jnp.bitwise_xor(me, d) for d in range(TEAM)]
    lane = lax.broadcasted_iota(jnp.int32, (8, LANES), 1)
    real_lane = lane < BINS
    sign = jnp.where(real_lane, 1.0 / windows, -1.0 / windows)
    tail = extended.shape[1] - planes * span
    if tail:
        extended[:, planes * span :, :] = jnp.zeros((windows, tail, LANES), jnp.float32)

    for n in range(len(halves)):
        for d, ref in enumerate(pieces[0][n]):
            for w in range(windows):
                side[w, d * count : (d + 1) * count, :] = ref[w * count : (w + 1) * count, :].astype(jnp.float32)
        for plane in range(planes):
            for d, ref in enumerate(pieces[len(sizes) - planes + plane][n]):
                start = pl.multiple_of(plane * span + blocks[d] * count, count)
                for w in range(windows):
                    extended[w, pl.ds(start, count), :] = ref[w * count : (w + 1) * count, :].astype(jnp.float32)

        def group(step, carry):
            at = pl.multiple_of(step * 8, 8)
            d = step // (count // 8)
            within = lax.rem(step, count // 8) * 8
            channel = jnp.bitwise_xor(me, d) * count + within
            straight, turned = [], []
            for w in range(windows):
                value = side[w, pl.ds(at, 8), :]
                straight.append(value * (1.0 / windows))
                turned.append(pltpu.roll(value, BINS, 1) * sign)
            for j in range(number):
                place = channel + offsets[first + j] - low * span
                real_part, imag_part = None, None
                for w in range(windows):
                    partner = extended[w, pl.ds(place, 8), :]
                    r, i = straight[w] * partner, turned[w] * partner
                    real_part = r if w == 0 else real_part + r
                    imag_part = i if w == 0 else imag_part + i
                folded = pltpu.roll(jnp.where(real_lane, imag_part, real_part), BINS, 1)
                both = jnp.where(real_lane, real_part, imag_part) + folded
                paired[d, pl.ds(within * pitch + j, 8, stride=pitch), :] = both
            return carry

        lax.fori_loop(0, span // 8, group, 0, unroll=True)
        for d in range(TEAM):
            out = outs[d - 1].at[0] if apart and d > 1 else outs[d // 2].at[2 * n + d % 2]
            for k in range(0, count, 2):
                rows = [paired[d, (k + m) * pitch : (k + m) * pitch + number, :] for m in range(2)]
                out[k * number : (k + 2) * number, :] = jnp.concatenate(rows, axis=0).astype(jnp.bfloat16)


def cross(windows, count, halves, first, last, offsets, team_planes, apart=False):
    span = TEAM * count
    stride = BAND // offsets.shape[0]
    low = (first * stride + 1) // span
    high = (span - 1 + last * stride) // span
    top = min(high, len(team_planes) - 1)
    used = [0] * (low > 0) + list(range(low, top + 1))
    groups = []
    for plane in (team_planes[p] for p in used):
        split = len(plane) > HALVES
        groups.append([plane[0]] * split + [plane[split + half] for half in halves])
    sizes = tuple(len(g) for g in groups)
    shares = [2 * len(halves)] * 2 if not apart else [2, 1, 1]
    given = [c for g in groups for c in g]
    number = last - first
    vmem = pl.BlockSpec(memory_space=pltpu.VMEM)
    return pl.pallas_call(
        functools.partial(cross_kernel, windows, count, halves, sizes, first, last, low, top - low + 1, int(apart)),
        in_specs=[pl.BlockSpec(memory_space=pltpu.SMEM)] + [vmem] * len(given),
        out_specs=[vmem] * len(shares),
        out_shape=[pltpu.VMEM((n, count * number, LANES), jnp.bfloat16) for n in shares],
        scratch_shapes=[
            pltpu.VMEM((windows, span, LANES), jnp.float32),
            pltpu.VMEM((windows, (high - low + 1) * span, LANES), jnp.float32),
            pltpu.VMEM((TEAM, count * (number + 1), LANES), jnp.float32),
        ],
        compiler_params=pltpu.CompilerParams(vmem_limit_bytes=8 * MIB),
        cost_estimate=busy(0.5 * len(halves)),
        name="cross",
    )(offsets, *given)


def lag_sum(pieces, table, half, columns):
    me = lax.rem(lax.axis_index("chan"), TEAM)
    odd = lax.rem(me, 2) == 1
    total = None
    for chip in range(TEAM // 2):
        first, second = pieces[2 * chip], pieces[2 * chip + 1]
        left = jnp.concatenate([jnp.where(odd, second, first), jnp.where(odd, first, second)], axis=1)
        right = table[half, jnp.bitwise_xor(me // 2, chip), :, columns]
        term = jnp.dot(left, right, preferred_element_type=jnp.float32)
        total = term if chip == 0 else total + term
    return total * (1.0 / math.sqrt(F))


def early_kernel(tile, *refs):
    low, high, (table, lower, upper) = refs[: HALVES * TEAM], refs[HALVES * TEAM : -3], refs[-3:]
    for t in range(LAGS // tile):
        columns = pl.ds(t * tile, tile)
        shares = [lag_sum([low[h * TEAM + d][d % 2] for d in range(TEAM)], table, h, columns) for h in range(HALVES)]
        lower[:, columns] = shares[0] + shares[1]
        upper[:, columns] = lag_sum([high[d][d % 2] for d in range(TEAM)], table, 0, columns)


def late_kernel(count, tile, *refs):
    high, (table, lower, upper, out, held, sems) = refs[:TEAM], refs[TEAM:]
    copies = []
    for t in range(LAGS // tile):
        columns = pl.ds(t * tile, tile)
        rest = lag_sum([high[d][min(d % 2, high[d].shape[0] - 1)] for d in range(TEAM)], table, 1, columns)
        both = [lower[:, columns], upper[:, columns] + rest]
        both = [v.reshape(count, v.shape[0] // count, tile) for v in both]
        held[t] = jnp.concatenate(both, axis=1).astype(jnp.bfloat16)
        copies.append(pltpu.make_async_copy(held.at[t], out.at[:, :, columns], sems.at[t]))
        copies[-1].start()
    for copy in copies:
        copy.wait()


def lags_early(low, high, table):
    vmem = pl.BlockSpec(memory_space=pltpu.VMEM)
    return pl.pallas_call(
        functools.partial(early_kernel, 512),
        in_specs=[vmem] * (len(low) + len(high) + 1),
        out_specs=[vmem] * 2,
        out_shape=[pltpu.VMEM((v[0].shape[1], LAGS), jnp.float32) for v in (low, high)],
        compiler_params=pltpu.CompilerParams(vmem_limit_bytes=12 * MIB),
        cost_estimate=busy(0.1),
        name="lags_early",
    )(*low, *high, table)


def lags_late(high, table, lower, upper, count, number):
    vmem = pl.BlockSpec(memory_space=pltpu.VMEM)
    tile = 512
    return pl.pallas_call(
        functools.partial(late_kernel, count, tile),
        in_specs=[vmem] * (TEAM + 3),
        out_specs=pl.BlockSpec(memory_space=pltpu.HBM),
        out_shape=jax.ShapeDtypeStruct((count, number, LAGS), jnp.bfloat16),
        scratch_shapes=[
            pltpu.VMEM((LAGS // tile, count, number, tile), jnp.bfloat16),
            pltpu.SemaphoreType.DMA((LAGS // tile,)),
        ],
        compiler_params=pltpu.CompilerParams(vmem_limit_bytes=16 * MIB),
        cost_estimate=busy(2.0),
        name="lags_late",
    )(*high, table, lower, upper)


def solution(mesh):
    ring = mesh.shape["chan"]
    if ring % TEAM:
        raise ValueError("chan")

    def after(value, *others):
        return lax.optimization_barrier((value,) + others)[0] if others else value

    def swapped(value, by):
        return lax.ppermute(value, "chan", [(i, i ^ by) for i in range(ring)])

    def down(value, hops):
        pairs = [(i, i - TEAM) for i in range(TEAM, ring) if i // TEAM + hops - 1 < ring // TEAM]
        return lax.ppermute(value, "chan", pairs)

    def shards(records, live_mask, offsets):
        count, windows, length = records.shape
        span = TEAM * count
        number = offsets.shape[0]
        forward, inverse = tables(length)
        mine, sibling, far0, far1 = spectra(records, live_mask, jnp.asarray(forward))
        inverse = jnp.asarray(inverse)
        near = joined(mine, swapped(sibling, 1))
        across = [swapped(far, 2) for far in (far0, far1)]
        own = [near] + [far_joined(c, swapped(c, 1)) for c in across]
        reach = min((span + BAND - 2) // span, ring // TEAM - 1)
        middle = number // 2

        def crossed(halves, first, last, planes, others=(), before=()):
            planes = [[after(planes[0][0], *others)] + planes[0][1:]] + planes[1:]
            near, far = cross(windows, count, halves, first, last, offsets, planes)
            return near, swapped(after(far, *before), 2)

        def gathered(near, back, *others):
            return near, swapped(near, 1), back, swapped(after(back, *others), 1)

        chunks = [own]
        low = []
        for hops in range(1, reach + 1):
            arrived = [down(c, hops) for c in chunks[-1]]
            if hops == JOIN:
                first = team_joined(0, arrived[0], arrived[1])
                low = [crossed((0,), 0, middle, chunks + [[first, None]])]
                arrived = [first, team_joined(1, arrived[0], after(arrived[2], low[0][0]))]
            chunks.append(arrived)
        for half in range(len(low), HALVES):
            low.append(crossed((half,), 0, middle, chunks))
        near0, back0 = crossed((0,), middle, number, chunks)
        near1, across1, diagonal1 = cross(windows, count, (1,), middle, number, offsets, chunks, True)
        low = gathered(*low[0], near0) + gathered(*low[1], near0)
        high = gathered(near0, back0, near1)
        lower, upper = lags_early(low, high, inverse)
        rest = near1, swapped(near1, 1), swapped(across1, 2), swapped(diagonal1, 3)
        return lags_late(rest, inverse, lower, upper, count, number)

    in_specs = (P(("day", "chan"), None, None), P(("day", "chan")), P())
    out_specs = P(("day", "chan"), None, None)
    return jax.shard_map(shards, mesh=mesh, in_specs=in_specs, out_specs=out_specs, check_vma=False)
```

```python
import functools
import math

import jax
import jax.numpy as jnp
import ml_dtypes
import numpy as np
from jax import lax
from jax.experimental import pallas as pl
from jax.experimental.pallas import tpu as pltpu
from jax.sharding import PartitionSpec as P

F = 512
F0 = 6
LAGS = 2048
BAND = 512
TEAM = 4
HALVES = 2
LANES = 128
BINS = F // (TEAM * HALVES)
QUADRANTS = 4

MIB = 1024 * 1024
JOIN = 2


def busy(microseconds):
    return pl.CostEstimate(flops=int(microseconds * 1.1535e9), bytes_accessed=0, transcendentals=0)


def column_order():
    kinds = np.asarray([0, 2, 1, 3])[(F0 + np.arange(F)) % QUADRANTS]
    bins = np.argsort(kinds, kind="stable").reshape(TEAM, HALVES, 1, BINS)
    parts = np.arange(2).reshape(1, 1, 2, 1) * F
    return (bins + parts).reshape(-1)


def tables(length):
    freqs = F0 + np.arange(F, dtype=np.int64)
    unit = np.float32(2.0 * math.pi / length)

    def cut(phase):
        angle = unit * np.mod(phase, length).astype(np.float32)
        return np.cos(angle), -np.sin(angle)

    order = column_order()
    part = length // QUADRANTS
    forward = np.concatenate(cut(np.arange(part)[:, None] * freqs[None, :]), axis=1)[:, order]
    forward = forward.reshape(part, 2, F).transpose(1, 0, 2)
    shifts = np.arange(LAGS, dtype=np.int64) - LAGS // 2
    inverse = np.concatenate(cut(freqs[:, None] * shifts[None, :]), axis=0)[order]
    inverse = inverse.reshape(TEAM, HALVES, LANES, LAGS).transpose(1, 0, 2, 3).reshape(HALVES, TEAM // 2, 2 * LANES, LAGS)
    return forward.astype(ml_dtypes.bfloat16), inverse.astype(ml_dtypes.bfloat16)


def spectra_kernel(windows, records_hbm, table_hbm, live_hbm, mine, sibling, far0, far1, records, table, live, spec, scales, sems):
    rows, length = records.shape
    count = rows // windows
    part = length // QUADRANTS
    pitch = windows + 1
    pairs = [(records_hbm, records), (table_hbm.at[0], table.at[0]), (table_hbm.at[1], table.at[1]), (live_hbm, live)]
    copies = [pltpu.make_async_copy(a, b, sems.at[n]) for n, (a, b) in enumerate(pairs)]
    for copy in copies:
        copy.start()
    me = lax.rem(lax.axis_index("chan"), TEAM)
    real_lane = lax.broadcasted_iota(jnp.int32, (rows, LANES), 1) < BINS
    copies[0].wait()
    x0, x1, x2, x3 = (records[:, q * part : (q + 1) * part] for q in range(QUADRANTS))

    def both(first, second, columns):
        total = jnp.dot(first, columns, preferred_element_type=jnp.float32)
        return total + jnp.dot(second, columns, preferred_element_type=jnp.float32)

    squares = jnp.zeros((rows, LANES), jnp.float32)
    for odd in range(2):
        copies[1 + odd].wait()
        columns = table[odd]
        if odd:
            left, right = both(x0, -x2, columns), both(x1, -x3, columns)
        else:
            left, right = both(x0, x2, columns), both(x1, x3, columns)
        for c in range(2):
            for half in range(HALVES):
                at = (c * HALVES + half) * LANES
                near, other = left[:, at : at + LANES], right[:, at : at + LANES]
                if odd:
                    other = pltpu.roll(other, BINS, 1)
                    value = near + jnp.where(real_lane == (c == 0), other, -other)
                else:
                    value = near + other if c == 0 else near - other
                squares = squares + value * value
                for channel in range(count):
                    rows_of = slice(channel * windows, (channel + 1) * windows)
                    spec[(2 * odd + c) * HALVES + half, channel * pitch : channel * pitch + windows, :] = value[rows_of]
    copies[3].wait()
    channel = lax.broadcasted_iota(jnp.int32, (rows, count), 0) // windows
    lane = lax.broadcasted_iota(jnp.int32, (rows, count), 1)
    mask = jnp.where(channel == lane, live[...].astype(jnp.float32), 0.0)
    gain = jnp.sum(mask, axis=1, keepdims=True)
    power = jnp.sum(squares, axis=1, keepdims=True)
    scale = jnp.broadcast_to(gain * lax.rsqrt(power * (1.0 / (2 * F)) + 1e-06), (rows, LANES))
    for channel in range(count):
        scales[channel * pitch : channel * pitch + windows, :] = scale[channel * windows : (channel + 1) * windows]
    for w in range(windows):
        every = pl.ds(w, count, stride=pitch)
        factor = scales[every, :]
        for half, far in enumerate((far0, far1)):
            places = [mine.at[half], sibling.at[half], far.at[0], far.at[1]]
            for d, place in enumerate(places):
                quarter = jnp.bitwise_xor(me, d)
                piece = spec[quarter * HALVES + half, every, :] * factor
                place[w * count : (w + 1) * count, :] = piece.astype(jnp.bfloat16)


def spectra(records, live_mask, table):
    count, windows, length = records.shape
    rows = count * windows
    return pl.pallas_call(
        functools.partial(spectra_kernel, windows),
        in_specs=[
            pl.BlockSpec(memory_space=pl.ANY),
            pl.BlockSpec(memory_space=pl.ANY),
            pl.BlockSpec(memory_space=pl.ANY),
        ],
        out_specs=[pl.BlockSpec(memory_space=pltpu.VMEM)] * 4,
        out_shape=[pltpu.VMEM((2, rows, LANES), jnp.bfloat16)] * 4,
        scratch_shapes=[
            pltpu.VMEM((rows, length), jnp.bfloat16),
            pltpu.VMEM(table.shape, jnp.bfloat16),
            pltpu.VMEM((1, count), jnp.int32),
            pltpu.VMEM((TEAM * HALVES, count * (windows + 1), LANES), jnp.float32),
            pltpu.VMEM((count * (windows + 1), LANES), jnp.float32),
            pltpu.SemaphoreType.DMA((4,)),
        ],
        compiler_params=pltpu.CompilerParams(vmem_limit_bytes=58 * MIB),
        cost_estimate=busy(3.0),
        name="spectra",
    )(records.reshape(rows, length), table, live_mask.reshape(1, count))


def join_kernel(first, second, out):
    for half in range(out.shape[0] // 2):
        out[2 * half] = first[half]
        out[2 * half + 1] = second[half]


def joined(first, second):
    vmem = pl.BlockSpec(memory_space=pltpu.VMEM)
    return pl.pallas_call(
        join_kernel,
        in_specs=[vmem] * 2,
        out_specs=vmem,
        out_shape=pltpu.VMEM((2 * first.shape[0],) + first.shape[1:], first.dtype),
        compiler_params=pltpu.CompilerParams(vmem_limit_bytes=2 * MIB),
        cost_estimate=busy(0.3),
        name="joined",
    )(first, second)


def team_kernel(half, near, far, out):
    for d in range(2):
        out[d] = near[2 * half + d]
        out[2 + d] = far[d]


def team_joined(half, near, far):
    vmem = pl.BlockSpec(memory_space=pltpu.VMEM)
    return pl.pallas_call(
        functools.partial(team_kernel, half),
        in_specs=[vmem] * 2,
        out_specs=vmem,
        out_shape=pltpu.VMEM((TEAM,) + far.shape[1:], far.dtype),
        compiler_params=pltpu.CompilerParams(vmem_limit_bytes=2 * MIB),
        cost_estimate=busy(0.3),
        name="team_joined",
    )(near, far)


def far_kernel(straight, crossed, out):
    out[0] = straight[0]
    out[1] = crossed[1]


def far_joined(straight, crossed):
    vmem = pl.BlockSpec(memory_space=pltpu.VMEM)
    return pl.pallas_call(
        far_kernel,
        in_specs=[vmem] * 2,
        out_specs=vmem,
        out_shape=pltpu.VMEM(straight.shape, straight.dtype),
        compiler_params=pltpu.CompilerParams(vmem_limit_bytes=2 * MIB),
        cost_estimate=busy(0.3),
        name="far_joined",
    )(straight, crossed)


def cross_kernel(windows, count, halves, sizes, first, last, low, planes, apart, offsets, *refs):
    outs, (side, extended, paired) = refs[-5 - apart : -3], refs[-3:]
    given = list(refs[: -5 - apart])
    pieces = []
    for size in sizes:
        arrays, given = given[:size], given[size:]
        if size == len(halves):
            pieces.append([[a.at[d] for d in range(TEAM)] for a in arrays])
        else:
            pieces.append([[arrays[0].at[2 * h + d] for d in range(2)] + [a.at[d] for d in range(2)] for h, a in zip(halves, arrays[1:])])
    me = lax.rem(lax.axis_index("chan"), TEAM)
    span = TEAM * count
    number = last - first
    pitch = number + 1
    blocks = [jnp.bitwise_xor(me, d) for d in range(TEAM)]
    lane = lax.broadcasted_iota(jnp.int32, (8, LANES), 1)
    real_lane = lane < BINS
    sign = jnp.where(real_lane, 1.0 / windows, -1.0 / windows)
    tail = extended.shape[1] - planes * span
    if tail:
        extended[:, planes * span :, :] = jnp.zeros((windows, tail, LANES), jnp.float32)

    for n in range(len(halves)):
        for d, ref in enumerate(pieces[0][n]):
            for w in range(windows):
                side[w, d * count : (d + 1) * count, :] = ref[w * count : (w + 1) * count, :].astype(jnp.float32)
        for plane in range(planes):
            for d, ref in enumerate(pieces[len(sizes) - planes + plane][n]):
                start = pl.multiple_of(plane * span + blocks[d] * count, count)
                for w in range(windows):
                    extended[w, pl.ds(start, count), :] = ref[w * count : (w + 1) * count, :].astype(jnp.float32)

        def group(step, carry):
            at = pl.multiple_of(step * 8, 8)
            d = step // (count // 8)
            within = lax.rem(step, count // 8) * 8
            channel = jnp.bitwise_xor(me, d) * count + within
            straight, turned = [], []
            for w in range(windows):
                value = side[w, pl.ds(at, 8), :]
                straight.append(value * (1.0 / windows))
                turned.append(pltpu.roll(value, BINS, 1) * sign)
            for j in range(number):
                place = channel + offsets[first + j] - low * span
                real_part, imag_part = None, None
                for w in range(windows):
                    partner = extended[w, pl.ds(place, 8), :]
                    r, i = straight[w] * partner, turned[w] * partner
                    real_part = r if w == 0 else real_part + r
                    imag_part = i if w == 0 else imag_part + i
                folded = pltpu.roll(jnp.where(real_lane, imag_part, real_part), BINS, 1)
                both = jnp.where(real_lane, real_part, imag_part) + folded
                paired[d, pl.ds(within * pitch + j, 8, stride=pitch), :] = both
            return carry

        lax.fori_loop(0, span // 8, group, 0, unroll=True)
        for d in range(TEAM):
            out = outs[d - 1].at[0] if apart and d > 1 else outs[d // 2].at[2 * n + d % 2]
            for k in range(0, count, 2):
                rows = [paired[d, (k + m) * pitch : (k + m) * pitch + number, :] for m in range(2)]
                out[k * number : (k + 2) * number, :] = jnp.concatenate(rows, axis=0).astype(jnp.bfloat16)


def cross(windows, count, halves, first, last, offsets, team_planes, apart=False):
    span = TEAM * count
    stride = BAND // offsets.shape[0]
    low = (first * stride + 1) // span
    high = (span - 1 + last * stride) // span
    top = min(high, len(team_planes) - 1)
    used = [0] * (low > 0) + list(range(low, top + 1))
    groups = []
    for plane in (team_planes[p] for p in used):
        split = len(plane) > HALVES
        groups.append([plane[0]] * split + [plane[split + half] for half in halves])
    sizes = tuple(len(g) for g in groups)
    shares = [2 * len(halves)] * 2 if not apart else [2, 1, 1]
    given = [c for g in groups for c in g]
    number = last - first
    vmem = pl.BlockSpec(memory_space=pltpu.VMEM)
    return pl.pallas_call(
        functools.partial(cross_kernel, windows, count, halves, sizes, first, last, low, top - low + 1, int(apart)),
        in_specs=[pl.BlockSpec(memory_space=pltpu.SMEM)] + [vmem] * len(given),
        out_specs=[vmem] * len(shares),
        out_shape=[pltpu.VMEM((n, count * number, LANES), jnp.bfloat16) for n in shares],
        scratch_shapes=[
            pltpu.VMEM((windows, span, LANES), jnp.float32),
            pltpu.VMEM((windows, (high - low + 1) * span, LANES), jnp.float32),
            pltpu.VMEM((TEAM, count * (number + 1), LANES), jnp.float32),
        ],
        compiler_params=pltpu.CompilerParams(vmem_limit_bytes=8 * MIB),
        cost_estimate=busy(0.5 * len(halves)),
        name="cross",
    )(offsets, *given)


def lag_sum(pieces, table, half, columns):
    me = lax.rem(lax.axis_index("chan"), TEAM)
    odd = lax.rem(me, 2) == 1
    total = None
    for chip in range(TEAM // 2):
        first, second = pieces[2 * chip], pieces[2 * chip + 1]
        left = jnp.concatenate([jnp.where(odd, second, first), jnp.where(odd, first, second)], axis=1)
        right = table[half, jnp.bitwise_xor(me // 2, chip), :, columns]
        term = jnp.dot(left, right, preferred_element_type=jnp.float32)
        total = term if chip == 0 else total + term
    return total * (1.0 / math.sqrt(F))


def early_kernel(tile, *refs):
    low, high, (table, lower, upper) = refs[: HALVES * TEAM], refs[HALVES * TEAM : -3], refs[-3:]
    for t in range(LAGS // tile):
        columns = pl.ds(t * tile, tile)
        shares = [lag_sum([low[h * TEAM + d][d % 2] for d in range(TEAM)], table, h, columns) for h in range(HALVES)]
        lower[:, columns] = shares[0] + shares[1]
        upper[:, columns] = lag_sum([high[d][d % 2] for d in range(TEAM)], table, 0, columns)


def late_kernel(count, tile, *refs):
    high, (table, lower, upper, out, held, sems) = refs[:TEAM], refs[TEAM:]
    copies = []
    for t in range(LAGS // tile):
        columns = pl.ds(t * tile, tile)
        rest = lag_sum([high[d][min(d % 2, high[d].shape[0] - 1)] for d in range(TEAM)], table, 1, columns)
        both = [lower[:, columns], upper[:, columns] + rest]
        both = [v.reshape(count, v.shape[0] // count, tile) for v in both]
        held[t] = jnp.concatenate(both, axis=1).astype(jnp.bfloat16)
        copies.append(pltpu.make_async_copy(held.at[t], out.at[:, :, columns], sems.at[t]))
        copies[-1].start()
    for copy in copies:
        copy.wait()


def lags_early(low, high, table):
    vmem = pl.BlockSpec(memory_space=pltpu.VMEM)
    return pl.pallas_call(
        functools.partial(early_kernel, 512),
        in_specs=[vmem] * (len(low) + len(high) + 1),
        out_specs=[vmem] * 2,
        out_shape=[pltpu.VMEM((v[0].shape[1], LAGS), jnp.float32) for v in (low, high)],
        compiler_params=pltpu.CompilerParams(vmem_limit_bytes=12 * MIB),
        cost_estimate=busy(0.1),
        name="lags_early",
    )(*low, *high, table)


def lags_late(high, table, lower, upper, count, number):
    vmem = pl.BlockSpec(memory_space=pltpu.VMEM)
    tile = 512
    return pl.pallas_call(
        functools.partial(late_kernel, count, tile),
        in_specs=[vmem] * (TEAM + 3),
        out_specs=pl.BlockSpec(memory_space=pltpu.HBM),
        out_shape=jax.ShapeDtypeStruct((count, number, LAGS), jnp.bfloat16),
        scratch_shapes=[
            pltpu.VMEM((LAGS // tile, count, number, tile), jnp.bfloat16),
            pltpu.SemaphoreType.DMA((LAGS // tile,)),
        ],
        compiler_params=pltpu.CompilerParams(vmem_limit_bytes=16 * MIB),
        cost_estimate=busy(2.0),
        name="lags_late",
    )(*high, table, lower, upper)


def solution(mesh):
    ring = mesh.shape["chan"]
    if ring % TEAM:
        raise ValueError("chan")

    def after(value, *others):
        return lax.optimization_barrier((value,) + others)[0] if others else value

    def swapped(value, by):
        return lax.ppermute(value, "chan", [(i, i ^ by) for i in range(ring)])

    def down(value, hops):
        pairs = [(i, i - TEAM) for i in range(TEAM, ring) if i // TEAM + hops - 1 < ring // TEAM]
        return lax.ppermute(value, "chan", pairs)

    def shards(records, live_mask, offsets):
        count, windows, length = records.shape
        span = TEAM * count
        number = offsets.shape[0]
        forward, inverse = tables(length)
        mine, sibling, far0, far1 = spectra(records, live_mask, jnp.asarray(forward))
        inverse = jnp.asarray(inverse)
        near = joined(mine, swapped(sibling, 1))
        across = [swapped(far, 2) for far in (far0, far1)]
        own = [near] + [far_joined(c, swapped(c, 1)) for c in across]
        reach = min((span + BAND - 2) // span, ring // TEAM - 1)
        middle = number // 2

        def crossed(halves, first, last, planes, others=(), before=()):
            planes = [[after(planes[0][0], *others)] + planes[0][1:]] + planes[1:]
            near, far = cross(windows, count, halves, first, last, offsets, planes)
            return near, swapped(after(far, *before), 2)

        def gathered(near, back, *others):
            return near, swapped(after(near, *others), 1), back, swapped(after(back, *others), 1)

        lower_planes = (span - 1 + middle * (BAND // number)) // span
        chunks = [own]
        low = []
        for hops in range(1, reach + 1):
            last = chunks[-1]
            if hops == JOIN:
                last = [last[0], after(last[1], last[2]), last[2]]
            arrived = [down(c, hops) for c in last]
            early = hops == lower_planes and hops >= JOIN
            if hops == JOIN:
                first = team_joined(0, arrived[0], arrived[1])
            elif hops > JOIN:
                first = arrived[0]
            if early:
                low = [crossed((0,), 0, middle, chunks + [[first, None]])]
                arrived[-1] = after(arrived[-1], low[0][0])
            if hops == JOIN:
                arrived = [first, team_joined(1, arrived[0], arrived[2])]
            chunks.append(arrived)
        for half in range(len(low), HALVES):
            low.append(crossed((half,), 0, middle, chunks))
        near0, back0 = crossed((0,), middle, number, chunks)
        near1, across1, diagonal1 = cross(windows, count, (1,), middle, number, offsets, chunks, True)
        low = gathered(*low[0]) + gathered(*low[1])
        high = gathered(near0, back0, near1)
        lower, upper = lags_early(low, high, inverse)
        rest = near1, swapped(near1, 1), swapped(across1, 2), swapped(diagonal1, 3)
        return lags_late(rest, inverse, lower, upper, count, number)

    in_specs = (P(("day", "chan"), None, None), P(("day", "chan")), P())
    out_specs = P(("day", "chan"), None, None)
    return jax.shard_map(shards, mesh=mesh, in_specs=in_specs, out_specs=out_specs, check_vma=False)
```

```python
import functools
import math

import jax
import jax.numpy as jnp
import ml_dtypes
import numpy as np
from jax import lax
from jax.experimental import pallas as pl
from jax.experimental.pallas import tpu as pltpu
from jax.sharding import PartitionSpec as P

F = 512
F0 = 6
LAGS = 2048
BAND = 512
TEAM = 4
HALVES = 2
LANES = 128
BINS = F // (TEAM * HALVES)
QUADRANTS = 4

MIB = 1024 * 1024
JOIN = 2


def busy(microseconds):
    return pl.CostEstimate(flops=int(microseconds * 1.1535e9), bytes_accessed=0, transcendentals=0)


def column_order():
    kinds = np.asarray([0, 2, 1, 3])[(F0 + np.arange(F)) % QUADRANTS]
    bins = np.argsort(kinds, kind="stable").reshape(TEAM, HALVES, 1, BINS)
    parts = np.arange(2).reshape(1, 1, 2, 1) * F
    return (bins + parts).reshape(-1)


def tables(length):
    freqs = F0 + np.arange(F, dtype=np.int64)
    unit = np.float32(2.0 * math.pi / length)

    def cut(phase):
        angle = unit * np.mod(phase, length).astype(np.float32)
        return np.cos(angle), -np.sin(angle)

    order = column_order()
    part = length // QUADRANTS
    forward = np.concatenate(cut(np.arange(part)[:, None] * freqs[None, :]), axis=1)[:, order]
    forward = forward.reshape(part, 2, F).transpose(1, 0, 2)
    shifts = np.arange(LAGS, dtype=np.int64) - LAGS // 2
    inverse = np.concatenate(cut(freqs[:, None] * shifts[None, :]), axis=0)[order]
    inverse = inverse.reshape(TEAM, HALVES, LANES, LAGS).transpose(1, 0, 2, 3).reshape(HALVES, TEAM // 2, 2 * LANES, LAGS)
    return forward.astype(ml_dtypes.bfloat16), inverse.astype(ml_dtypes.bfloat16)


def spectra_kernel(windows, records_hbm, table_hbm, live_hbm, mine, sibling, far0, far1, records, table, live, spec, scales, sems):
    rows, length = records.shape
    count = rows // windows
    part = length // QUADRANTS
    pitch = windows + 1
    pairs = [(records_hbm, records), (table_hbm.at[0], table.at[0]), (table_hbm.at[1], table.at[1]), (live_hbm, live)]
    copies = [pltpu.make_async_copy(a, b, sems.at[n]) for n, (a, b) in enumerate(pairs)]
    for copy in copies:
        copy.start()
    me = lax.rem(lax.axis_index("chan"), TEAM)
    real_lane = lax.broadcasted_iota(jnp.int32, (rows, LANES), 1) < BINS
    copies[0].wait()
    x0, x1, x2, x3 = (records[:, q * part : (q + 1) * part] for q in range(QUADRANTS))

    def both(first, second, columns):
        total = jnp.dot(first, columns, preferred_element_type=jnp.float32)
        return total + jnp.dot(second, columns, preferred_element_type=jnp.float32)

    squares = jnp.zeros((rows, LANES), jnp.float32)
    for odd in range(2):
        copies[1 + odd].wait()
        columns = table[odd]
        if odd:
            left, right = both(x0, -x2, columns), both(x1, -x3, columns)
        else:
            left, right = both(x0, x2, columns), both(x1, x3, columns)
        for c in range(2):
            for half in range(HALVES):
                at = (c * HALVES + half) * LANES
                near, other = left[:, at : at + LANES], right[:, at : at + LANES]
                if odd:
                    other = pltpu.roll(other, BINS, 1)
                    value = near + jnp.where(real_lane == (c == 0), other, -other)
                else:
                    value = near + other if c == 0 else near - other
                squares = squares + value * value
                for channel in range(count):
                    rows_of = slice(channel * windows, (channel + 1) * windows)
                    spec[(2 * odd + c) * HALVES + half, channel * pitch : channel * pitch + windows, :] = value[rows_of]
    copies[3].wait()
    channel = lax.broadcasted_iota(jnp.int32, (rows, count), 0) // windows
    lane = lax.broadcasted_iota(jnp.int32, (rows, count), 1)
    mask = jnp.where(channel == lane, live[...].astype(jnp.float32), 0.0)
    gain = jnp.sum(mask, axis=1, keepdims=True)
    power = jnp.sum(squares, axis=1, keepdims=True)
    scale = jnp.broadcast_to(gain * lax.rsqrt(power * (1.0 / (2 * F)) + 1e-06), (rows, LANES))
    for channel in range(count):
        scales[channel * pitch : channel * pitch + windows, :] = scale[channel * windows : (channel + 1) * windows]
    for w in range(windows):
        every = pl.ds(w, count, stride=pitch)
        factor = scales[every, :]
        for half, far in enumerate((far0, far1)):
            places = [mine.at[half], sibling.at[half], far.at[0], far.at[1]]
            for d, place in enumerate(places):
                quarter = jnp.bitwise_xor(me, d)
                piece = spec[quarter * HALVES + half, every, :] * factor
                place[w * count : (w + 1) * count, :] = piece.astype(jnp.bfloat16)


def spectra(records, live_mask, table):
    count, windows, length = records.shape
    rows = count * windows
    return pl.pallas_call(
        functools.partial(spectra_kernel, windows),
        in_specs=[
            pl.BlockSpec(memory_space=pl.ANY),
            pl.BlockSpec(memory_space=pl.ANY),
            pl.BlockSpec(memory_space=pl.ANY),
        ],
        out_specs=[pl.BlockSpec(memory_space=pltpu.VMEM)] * 4,
        out_shape=[pltpu.VMEM((2, rows, LANES), jnp.bfloat16)] * 4,
        scratch_shapes=[
            pltpu.VMEM((rows, length), jnp.bfloat16),
            pltpu.VMEM(table.shape, jnp.bfloat16),
            pltpu.VMEM((1, count), jnp.int32),
            pltpu.VMEM((TEAM * HALVES, count * (windows + 1), LANES), jnp.float32),
            pltpu.VMEM((count * (windows + 1), LANES), jnp.float32),
            pltpu.SemaphoreType.DMA((4,)),
        ],
        compiler_params=pltpu.CompilerParams(vmem_limit_bytes=58 * MIB),
        cost_estimate=busy(3.0),
        name="spectra",
    )(records.reshape(rows, length), table, live_mask.reshape(1, count))


def join_kernel(first, second, out):
    for half in range(out.shape[0] // 2):
        out[2 * half] = first[half]
        out[2 * half + 1] = second[half]


def joined(first, second):
    vmem = pl.BlockSpec(memory_space=pltpu.VMEM)
    return pl.pallas_call(
        join_kernel,
        in_specs=[vmem] * 2,
        out_specs=vmem,
        out_shape=pltpu.VMEM((2 * first.shape[0],) + first.shape[1:], first.dtype),
        compiler_params=pltpu.CompilerParams(vmem_limit_bytes=2 * MIB),
        cost_estimate=busy(0.3),
        name="joined",
    )(first, second)


def team_kernel(half, near, far, out):
    for d in range(2):
        out[d] = near[2 * half + d]
        out[2 + d] = far[d]


def team_joined(half, near, far):
    vmem = pl.BlockSpec(memory_space=pltpu.VMEM)
    return pl.pallas_call(
        functools.partial(team_kernel, half),
        in_specs=[vmem] * 2,
        out_specs=vmem,
        out_shape=pltpu.VMEM((TEAM,) + far.shape[1:], far.dtype),
        compiler_params=pltpu.CompilerParams(vmem_limit_bytes=2 * MIB),
        cost_estimate=busy(0.3),
        name="team_joined",
    )(near, far)


def far_kernel(straight, crossed, out):
    out[0] = straight[0]
    out[1] = crossed[1]


def far_joined(straight, crossed):
    vmem = pl.BlockSpec(memory_space=pltpu.VMEM)
    return pl.pallas_call(
        far_kernel,
        in_specs=[vmem] * 2,
        out_specs=vmem,
        out_shape=pltpu.VMEM(straight.shape, straight.dtype),
        compiler_params=pltpu.CompilerParams(vmem_limit_bytes=2 * MIB),
        cost_estimate=busy(0.3),
        name="far_joined",
    )(straight, crossed)


def cross_kernel(windows, count, halves, sizes, first, last, low, planes, apart, offsets, *refs):
    outs, (side, extended, paired) = refs[-5 - apart : -3], refs[-3:]
    given = list(refs[: -5 - apart])
    pieces = []
    for size in sizes:
        arrays, given = given[:size], given[size:]
        if size == len(halves):
            pieces.append([[a.at[d] for d in range(TEAM)] for a in arrays])
        else:
            pieces.append([[arrays[0].at[2 * h + d] for d in range(2)] + [a.at[d] for d in range(2)] for h, a in zip(halves, arrays[1:])])
    me = lax.rem(lax.axis_index("chan"), TEAM)
    span = TEAM * count
    number = last - first
    pitch = number + 1
    blocks = [jnp.bitwise_xor(me, d) for d in range(TEAM)]
    lane = lax.broadcasted_iota(jnp.int32, (8, LANES), 1)
    real_lane = lane < BINS
    sign = jnp.where(real_lane, 1.0 / windows, -1.0 / windows)
    tail = extended.shape[1] - planes * span
    if tail:
        extended[:, planes * span :, :] = jnp.zeros((windows, tail, LANES), jnp.float32)

    for n in range(len(halves)):
        for d, ref in enumerate(pieces[0][n]):
            for w in range(windows):
                side[w, d * count : (d + 1) * count, :] = ref[w * count : (w + 1) * count, :].astype(jnp.float32)
        for plane in range(planes):
            for d, ref in enumerate(pieces[len(sizes) - planes + plane][n]):
                start = pl.multiple_of(plane * span + blocks[d] * count, count)
                for w in range(windows):
                    extended[w, pl.ds(start, count), :] = ref[w * count : (w + 1) * count, :].astype(jnp.float32)

        def group(step, carry):
            at = pl.multiple_of(step * 8, 8)
            d = step // (count // 8)
            within = lax.rem(step, count // 8) * 8
            channel = jnp.bitwise_xor(me, d) * count + within
            straight, turned = [], []
            for w in range(windows):
                value = side[w, pl.ds(at, 8), :]
                straight.append(value * (1.0 / windows))
                turned.append(pltpu.roll(value, BINS, 1) * sign)
            for j in range(number):
                place = channel + offsets[first + j] - low * span
                real_part, imag_part = None, None
                for w in range(windows):
                    partner = extended[w, pl.ds(place, 8), :]
                    r, i = straight[w] * partner, turned[w] * partner
                    real_part = r if w == 0 else real_part + r
                    imag_part = i if w == 0 else imag_part + i
                folded = pltpu.roll(jnp.where(real_lane, imag_part, real_part), BINS, 1)
                both = jnp.where(real_lane, real_part, imag_part) + folded
                paired[d, pl.ds(within * pitch + j, 8, stride=pitch), :] = both
            return carry

        lax.fori_loop(0, span // 8, group, 0, unroll=True)
        for d in range(TEAM):
            out = outs[d - 1].at[0] if apart and d > 1 else outs[d // 2].at[2 * n + d % 2]
            for k in range(0, count, 2):
                rows = [paired[d, (k + m) * pitch : (k + m) * pitch + number, :] for m in range(2)]
                out[k * number : (k + 2) * number, :] = jnp.concatenate(rows, axis=0).astype(jnp.bfloat16)


def cross(windows, count, halves, first, last, offsets, team_planes, apart=False):
    span = TEAM * count
    stride = BAND // offsets.shape[0]
    low = (first * stride + 1) // span
    high = (span - 1 + last * stride) // span
    top = min(high, len(team_planes) - 1)
    used = [0] * (low > 0) + list(range(low, top + 1))
    groups = []
    for plane in (team_planes[p] for p in used):
        split = len(plane) > HALVES
        groups.append([plane[0]] * split + [plane[split + half] for half in halves])
    sizes = tuple(len(g) for g in groups)
    shares = [2 * len(halves)] * 2 if not apart else [2, 1, 1]
    given = [c for g in groups for c in g]
    number = last - first
    vmem = pl.BlockSpec(memory_space=pltpu.VMEM)
    return pl.pallas_call(
        functools.partial(cross_kernel, windows, count, halves, sizes, first, last, low, top - low + 1, int(apart)),
        in_specs=[pl.BlockSpec(memory_space=pltpu.SMEM)] + [vmem] * len(given),
        out_specs=[vmem] * len(shares),
        out_shape=[pltpu.VMEM((n, count * number, LANES), jnp.bfloat16) for n in shares],
        scratch_shapes=[
            pltpu.VMEM((windows, span, LANES), jnp.float32),
            pltpu.VMEM((windows, (high - low + 1) * span, LANES), jnp.float32),
            pltpu.VMEM((TEAM, count * (number + 1), LANES), jnp.float32),
        ],
        compiler_params=pltpu.CompilerParams(vmem_limit_bytes=8 * MIB),
        cost_estimate=busy(0.5 * len(halves)),
        name="cross",
    )(offsets, *given)


def lag_sum(pieces, table, half, columns):
    me = lax.rem(lax.axis_index("chan"), TEAM)
    odd = lax.rem(me, 2) == 1
    total = None
    for chip in range(TEAM // 2):
        first, second = pieces[2 * chip], pieces[2 * chip + 1]
        left = jnp.concatenate([jnp.where(odd, second, first), jnp.where(odd, first, second)], axis=1)
        right = table[half, jnp.bitwise_xor(me // 2, chip), :, columns]
        term = jnp.dot(left, right, preferred_element_type=jnp.float32)
        total = term if chip == 0 else total + term
    return total * (1.0 / math.sqrt(F))


def early_kernel(tile, *refs):
    low, high, (table, lower, upper) = refs[: HALVES * TEAM], refs[HALVES * TEAM : -3], refs[-3:]
    for t in range(LAGS // tile):
        columns = pl.ds(t * tile, tile)
        shares = [lag_sum([low[h * TEAM + d][d % 2] for d in range(TEAM)], table, h, columns) for h in range(HALVES)]
        lower[:, columns] = shares[0] + shares[1]
        upper[:, columns] = lag_sum([high[d][d % 2] for d in range(TEAM)], table, 0, columns)


def late_kernel(count, tile, *refs):
    high, (table, lower, upper, out, held, sems) = refs[:TEAM], refs[TEAM:]
    copies = []
    for t in range(LAGS // tile):
        columns = pl.ds(t * tile, tile)
        rest = lag_sum([high[d][min(d % 2, high[d].shape[0] - 1)] for d in range(TEAM)], table, 1, columns)
        both = [lower[:, columns], upper[:, columns] + rest]
        both = [v.reshape(count, v.shape[0] // count, tile) for v in both]
        held[t] = jnp.concatenate(both, axis=1).astype(jnp.bfloat16)
        copies.append(pltpu.make_async_copy(held.at[t], out.at[:, :, columns], sems.at[t]))
        copies[-1].start()
    for copy in copies:
        copy.wait()


def lags_early(low, high, table):
    vmem = pl.BlockSpec(memory_space=pltpu.VMEM)
    return pl.pallas_call(
        functools.partial(early_kernel, 512),
        in_specs=[vmem] * (len(low) + len(high) + 1),
        out_specs=[vmem] * 2,
        out_shape=[pltpu.VMEM((v[0].shape[1], LAGS), jnp.float32) for v in (low, high)],
        compiler_params=pltpu.CompilerParams(vmem_limit_bytes=12 * MIB),
        cost_estimate=busy(0.1),
        name="lags_early",
    )(*low, *high, table)


def lags_late(high, table, lower, upper, count, number):
    vmem = pl.BlockSpec(memory_space=pltpu.VMEM)
    tile = 256
    return pl.pallas_call(
        functools.partial(late_kernel, count, tile),
        in_specs=[vmem] * (TEAM + 3),
        out_specs=pl.BlockSpec(memory_space=pltpu.HBM),
        out_shape=jax.ShapeDtypeStruct((count, number, LAGS), jnp.bfloat16),
        scratch_shapes=[
            pltpu.VMEM((LAGS // tile, count, number, tile), jnp.bfloat16),
            pltpu.SemaphoreType.DMA((LAGS // tile,)),
        ],
        compiler_params=pltpu.CompilerParams(vmem_limit_bytes=16 * MIB),
        cost_estimate=busy(2.0),
        name="lags_late",
    )(*high, table, lower, upper)


def solution(mesh):
    ring = mesh.shape["chan"]
    if ring % TEAM:
        raise ValueError("chan")

    def after(value, *others):
        return lax.optimization_barrier((value,) + others)[0] if others else value

    def swapped(value, by):
        return lax.ppermute(value, "chan", [(i, i ^ by) for i in range(ring)])

    def down(value, hops):
        pairs = [(i, i - TEAM) for i in range(TEAM, ring) if i // TEAM + hops - 1 < ring // TEAM]
        return lax.ppermute(value, "chan", pairs)

    def shards(records, live_mask, offsets):
        count, windows, length = records.shape
        span = TEAM * count
        number = offsets.shape[0]
        forward, inverse = tables(length)
        mine, sibling, far0, far1 = spectra(records, live_mask, jnp.asarray(forward))
        inverse = jnp.asarray(inverse)
        near = joined(mine, swapped(sibling, 1))
        across = [swapped(far, 2) for far in (far0, far1)]
        own = [near] + [far_joined(c, swapped(c, 1)) for c in across]
        reach = min((span + BAND - 2) // span, ring // TEAM - 1)
        middle = number // 2

        def crossed(halves, first, last, planes, others=(), before=()):
            planes = [[after(planes[0][0], *others)] + planes[0][1:]] + planes[1:]
            near, far = cross(windows, count, halves, first, last, offsets, planes)
            return near, swapped(after(far, *before), 2)

        def gathered(near, back, *others):
            return near, swapped(after(near, *others), 1), back, swapped(after(back, *others), 1)

        lower_planes = (span - 1 + middle * (BAND // number)) // span
        chunks = [own]
        low = []
        for hops in range(1, reach + 1):
            last = chunks[-1]
            if hops == JOIN:
                last = [last[0], after(last[1], last[2]), last[2]]
            arrived = [down(c, hops) for c in last]
            early = hops == lower_planes and hops >= JOIN
            if hops == JOIN:
                first = team_joined(0, arrived[0], arrived[1])
            elif hops > JOIN:
                first = arrived[0]
            if early:
                low = [crossed((0,), 0, middle, chunks + [[first, None]])]
                arrived[-1] = after(arrived[-1], low[0][0])
            if hops == JOIN:
                arrived = [first, team_joined(1, arrived[0], arrived[2])]
            chunks.append(arrived)
        for half in range(len(low), HALVES):
            low.append(crossed((half,), 0, middle, chunks))
        near0, back0 = crossed((0,), middle, number, chunks)
        near1, across1, diagonal1 = cross(windows, count, (1,), middle, number, offsets, chunks, True)
        low = gathered(*low[0]) + gathered(*low[1])
        high = gathered(near0, back0, near1)
        lower, upper = lags_early(low, high, inverse)
        rest = near1, swapped(near1, 1), swapped(across1, 2), swapped(diagonal1, 3)
        return lags_late(rest, inverse, lower, upper, count, number)

    in_specs = (P(("day", "chan"), None, None), P(("day", "chan")), P())
    out_specs = P(("day", "chan"), None, None)
    return jax.shard_map(shards, mesh=mesh, in_specs=in_specs, out_specs=out_specs, check_vma=False)
```
